32 devices in a mesh: pipe: 4 (over y, x), seq: 8 (over z, core).
Axes of the slice: x: 2, y: 2, z: 4, core: 2. Of those that a mesh axis runs over, the one named last changes fastest.
Arguments:
- inputs: bfloat16 [4, 1024, 2048], P('pipe', 'seq'), may hold values from -6 to 6
- lengths: int32 [4, 32], replicated, may hold values from 1 to 128, 1024 in all within a row
- order: int32 [4], replicated, may hold values from 0 to 3, each once
- norm_gain: float32 [4, 2048], P('pipe'), may hold values from 0.25 to 1.75
- rate: float32 [4, 16, 2048], P('pipe'), may hold values from 0.004 to 0.15
- angle: float32 [4, 16, 2048], P('pipe'), may hold values from -3.140625 to 3.140625
- coef: float32 [4, 2, 16, 2048], P('pipe'), may hold values from -0.3 to 0.3
- skip: float32 [4, 2048], P('pipe'), may hold values from 0.5 to 1.5
- score_gains: float32 [4, 2, 2048], P('pipe'), may hold values from -3 to 4.6
- out_proj: bfloat16 [4, 2048, 2048], P('pipe', 'seq'), may hold values from -0.125 to 0.125
Outputs:
- outputs: bfloat16 [4, 1024, 2048], P('pipe', 'seq')
The draws below stay inside these ranges and needn't reach their ends.
Inputs may be any that keep to these rules, and one draw needn't show every extreme that they name: Each row of lengths sums to 1024, and every row holds a document of exactly 128 positions. `order`: each packed row appears once.
All inputs are finite; a program needn't handle non-finite values.
Results may differ from the reference program's by a relative error of at most 0.02.
The reference program's roundings to bfloat16 on the way count: a program that leaves them out, or rounds other values in their place, can miss the bound.
Values may be sent and summed in bfloat16 or wider, within the bound.
No kernel may reach another device: no remote copies, remote signals or barrier semaphores. Data moves between devices by JAX's collectives and lax.ppermute only.
A program may use at most 128 MiB of HBM per device.

```python
import math
import jax
import jax.numpy as jnp
import numpy as np
from jax import lax

D = 2048
HEAD_DIM = 128
MODES = 16
TOK_DEV = 128
SECTIONS = 4
MICRO = 4
TOKENS = 1024
DOCS = 32


def draw_score_gains(key, part):
    head_count = D // HEAD_DIM
    keys_all = jax.random.split(jax.random.fold_in(key, 17), 5)
    section_keys = jax.random.split(keys_all[0], SECTIONS)
    ranks = jax.vmap(lambda one_key: jax.random.permutation(one_key, head_count))(section_keys)
    spread_heads = (ranks < head_count // 2).astype(jnp.float32)
    spread_mask = jnp.repeat(spread_heads, HEAD_DIM, axis=1)
    flips = jax.random.bernoulli(keys_all[1], 0.5, (SECTIONS, D))
    signs = jnp.where(flips, 1.0, -1.0).astype(jnp.float32)
    sign_pair = jnp.stack([signs, jnp.ones_like(signs)], axis=1)
    aligned = jax.random.uniform(keys_all[2], (SECTIONS, 2, D), jnp.float32, 0.6, 1.6)
    magnitude = jax.random.uniform(keys_all[4], (SECTIONS, 2, D), jnp.float32, 1.2, 2.4)
    spread_gain = magnitude * sign_pair
    return jnp.where(spread_mask[:, None, :] > 0.5, spread_gain, aligned)


def shard_levels(stream_key, shape, pieces, low, high):
    factor_of = 1.0
    for position, blocks in pieces:
        steps = jax.random.uniform(jax.random.fold_in(jax.random.fold_in(stream_key, 6), position), (blocks,), jnp.float32, low / len(pieces), high / len(pieces))
        factor_of = factor_of * jnp.repeat(jnp.exp(steps), shape[position] // blocks).reshape((-1,) + (1,) * (len(shape) - 1 - position))
    return factor_of


def profile(amount, total, limit, lean):
    portions = [(1 << 20) // math.isqrt(standing ** lean) + 1 for standing in range(2, amount + 1)]
    spare, given = total - limit - (amount - 1), [1] * (amount - 1)
    while spare > 0:
        candidates = [i for i in range(amount - 1) if given[i] < limit]
        whole, budget = sum([portions[i] for i in candidates]), spare
        for i in candidates:
            more = min(limit - given[i], max(1, budget * portions[i] // whole), spare)
            given[i] = given[i] + more
            spare = spare - more
    return np.array([limit] + given)


def ragged(key, amount, total, limit, slope):
    if amount == 2:
        one = jax.random.randint(key, (), max(1, total - limit), min(limit, total - 1) + 1)
        return jnp.stack([one, total - one])
    sizes = jnp.asarray(profile(amount, total, limit, slope), jnp.int32)
    couples = (amount - 1) // 2
    giver, taker = sizes[1:1 + 2 * couples:2], sizes[2:2 + 2 * couples:2]
    slack = jnp.minimum(giver - 1, limit - taker)
    passed = jax.random.randint(jax.random.fold_in(key, 1), (couples,), 0, 1 << 20) % (slack + 1)
    sizes = sizes.at[1:1 + 2 * couples:2].set(giver - passed).at[2:2 + 2 * couples:2].set(taker + passed)
    return sizes[jax.random.permutation(jax.random.fold_in(key, 2), amount)]


def gaussian(own_key, extent, deviation, most, cuts=(), kind=jnp.bfloat16):
    loudness = shard_levels(own_key, extent, cuts, -0.22, 0.18) if cuts else 1.0
    entries = jax.random.normal(own_key, extent, jnp.float32) * deviation * loudness
    return jnp.minimum(jnp.maximum(entries, -most), most).astype(kind)


def setup_inputs(seed: int = 0) -> dict:
    keys = jax.random.split(jax.random.key(seed), 11)
    inputs = gaussian(keys[0], (MICRO, TOKENS, D), 1.0, 6.0, ((0, 4), (1, 8)))
    lengths = jax.vmap(lambda own: ragged(own, DOCS, TOKENS, TOK_DEV, 2))(jax.random.split(keys[1], MICRO)).reshape((MICRO, DOCS)).astype(jnp.int32)
    order = jax.random.permutation(keys[2], MICRO).astype(jnp.int32)
    norm_gain = jnp.clip(1.0 + 0.15 * jax.random.normal(keys[3], (SECTIONS, D), jnp.float32), 0.25, 1.75)
    rate = jnp.clip(jnp.exp(math.log(0.15) - 3.624341 * jax.random.uniform(keys[4], (SECTIONS, MODES, D), jnp.float32) ** shard_levels(keys[4], (SECTIONS, MODES, D), ((0, 4),), -0.2, 0.2)), 0.004, 0.15)
    angle = jnp.clip(jax.random.uniform(keys[5], (SECTIONS, MODES, D), jnp.float32, -3.140625, 3.140625), -3.140625, 3.140625)
    coef = gaussian(keys[6], (SECTIONS, 2, MODES, D), 0.05, 0.3, ((0, 4),), jnp.float32)
    skip = jnp.clip(0.5 + 1.0 * jax.random.uniform(keys[7], (SECTIONS, D), jnp.float32) ** shard_levels(keys[7], (SECTIONS, D), ((0, 4),), -0.2, 0.2), 0.5, 1.5)
    score_gains = draw_score_gains(jax.random.fold_in(keys[10], 71), 0)
    out_proj = gaussian(keys[9], (SECTIONS, D, D), D ** -0.5, 0.125, ((0, 4), (1, 8)))
    return dict(inputs=inputs, lengths=lengths, order=order, norm_gain=norm_gain, rate=rate, angle=angle, coef=coef, skip=skip, score_gains=score_gains, out_proj=out_proj)


inner_span = 16
norm_eps = 1e-06
masked_score = -1e+30
highest = lax.Precision.HIGHEST

def mode_powers(rate_now, angle_now, exponents):
    magnitude = jnp.exp(-exponents[:, None, None] * rate_now[None])
    turning = exponents[:, None, None] * angle_now[None]
    return (magnitude * jnp.cos(turning), magnitude * jnp.sin(turning))

def mode_tables(rate_now, angle_now, coef_now):
    lag_steps = jnp.arange(inner_span).astype(jnp.float32)
    coef_re = coef_now[0]
    coef_im = coef_now[1]
    power_re, power_im = mode_powers(rate_now, angle_now, lag_steps)
    kernel = 2.0 * lax.optimization_barrier(jnp.sum(coef_re[None] * power_re - coef_im[None] * power_im, axis=1))
    ahead_re, ahead_im = mode_powers(rate_now, angle_now, lag_steps + 1.0)
    carry_re = coef_re[None] * ahead_re - coef_im[None] * ahead_im
    carry_im = coef_re[None] * ahead_im + coef_im[None] * ahead_re
    back_re, back_im = mode_powers(rate_now, angle_now, inner_span - 1.0 - lag_steps)
    whole_re, whole_im = mode_powers(rate_now, angle_now, jnp.full((1,), 1.0 * inner_span, jnp.float32))
    return (kernel, carry_re, carry_im, back_re, back_im, whole_re[0], whole_im[0])

def local_conv(kernel, signal, doc_ids):
    result = kernel[0][None, None, :] * signal
    for lag_steps in range(1, inner_span):
        shifted = jnp.pad(signal[:, :-lag_steps], ((0, 0), (lag_steps, 0), (0, 0)))
        same_doc = jnp.pad(doc_ids[:, lag_steps:] == doc_ids[:, :-lag_steps], ((0, 0), (lag_steps, 0)))
        result = result + kernel[lag_steps][None, None, :] * shifted * same_doc[:, :, None].astype(shifted.dtype)
    return result

def rms_scaled(values):
    return values * lax.rsqrt(lax.optimization_barrier(jnp.mean(values * values, axis=1, keepdims=True)) + norm_eps)

def ssm_mix(scaled, doc_ids, tables_all, skip_now):
    kernel, carry_re, carry_im, back_re, back_im, whole_re, whole_im = tables_all
    block_count = scaled.shape[0] // inner_span
    blocks = scaled.reshape(block_count, inner_span, scaled.shape[1])
    block_docs = doc_ids.reshape(block_count, inner_span)
    prior_docs = jnp.concatenate([jnp.full((1,), -1, jnp.int32), block_docs[:-1, -1].astype(jnp.int32)])
    base_out = local_conv(kernel, blocks, block_docs) + skip_now * blocks

    def advance(carried, item):
        state_re, state_im = carried
        block_now, docs_now, prior_now = item
        entry_flags = (docs_now == prior_now).astype(block_now.dtype)
        reached = 2.0 * (jnp.einsum('tmd,md->td', carry_re, state_re, precision=highest) - jnp.einsum('tmd,md->td', carry_im, state_im, precision=highest))
        last_doc = docs_now[-1]
        kept_rows = block_now * (docs_now == last_doc).astype(block_now.dtype)[:, None]
        local_re = jnp.einsum('smd,sd->md', back_re, kept_rows, precision=highest)
        local_im = jnp.einsum('smd,sd->md', back_im, kept_rows, precision=highest)
        link_now = (last_doc == prior_now).astype(block_now.dtype)
        next_re = local_re + link_now * (whole_re * state_re - whole_im * state_im)
        next_im = local_im + link_now * (whole_re * state_im + whole_im * state_re)
        return ((next_re, next_im), entry_flags[:, None] * reached)
    zeros = jnp.zeros(whole_re.shape, jnp.float32)
    _, reached_all = lax.scan(advance, (zeros, zeros), (blocks, block_docs, prior_docs))
    return (base_out + reached_all).reshape(scaled.shape)

def block_attention(query_rows, key_rows, value_rows, residual, query_docs, key_docs, query_pos, key_pos, proj_now):
    row_count = query_rows.shape[0]
    query_heads = query_rows.astype(jnp.float32).reshape(row_count, -1, HEAD_DIM)
    key_heads = key_rows.astype(jnp.float32).reshape(key_rows.shape[0], -1, HEAD_DIM)
    value_heads = value_rows.astype(jnp.float32).reshape(value_rows.shape[0], -1, HEAD_DIM)
    scores = jnp.einsum('thd,shd->hts', query_heads, key_heads, precision=highest) * HEAD_DIM ** (-0.5)
    allowed = (key_pos[None, :] <= query_pos[:, None]) & (key_docs[None, :] == query_docs[:, None])
    scores = jnp.where(allowed[None], scores, masked_score)
    largest = lax.optimization_barrier(jnp.max(scores, axis=2, keepdims=True))
    raw_weights = jnp.exp(scores - largest)
    weights = (raw_weights / lax.optimization_barrier(jnp.sum(raw_weights, axis=2, keepdims=True))).astype(jnp.bfloat16)
    attended = jnp.einsum('hts,shd->thd', weights.astype(jnp.float32), value_heads, precision=highest)
    attended = attended.reshape(row_count, -1).astype(jnp.bfloat16)
    projected = jnp.dot(attended, proj_now, preferred_element_type=jnp.float32)
    return (residual.astype(jnp.float32) + projected).astype(jnp.bfloat16)

def doc_attention(middle, doc_ids, gains_now, proj_now):
    total_rows = middle.shape[0]
    normed = rms_scaled(middle.astype(jnp.float32))
    queries = (normed * gains_now[0]).astype(jnp.bfloat16)
    key_rows = (normed * gains_now[1]).astype(jnp.bfloat16)
    padding = jnp.zeros((TOK_DEV, middle.shape[1]), jnp.bfloat16)
    keys_padded = jnp.concatenate([padding, key_rows])
    values_padded = jnp.concatenate([padding, middle])
    docs_padded = jnp.concatenate([jnp.full((TOK_DEV,), -1, jnp.int32), doc_ids.astype(jnp.int32)])
    pos_padded = (jnp.arange(total_rows + TOK_DEV) - TOK_DEV).astype(jnp.int32)

    def one_block(index):
        first = (index * TOK_DEV).astype(jnp.int32)
        own_first = (first + TOK_DEV).astype(jnp.int32)
        query_rows = lax.dynamic_slice_in_dim(queries, first, TOK_DEV, 0)
        residual = lax.dynamic_slice_in_dim(middle, first, TOK_DEV, 0)
        key_now = lax.dynamic_slice_in_dim(keys_padded, first, 2 * TOK_DEV, 0)
        value_now = lax.dynamic_slice_in_dim(values_padded, first, 2 * TOK_DEV, 0)
        key_docs = lax.dynamic_slice_in_dim(docs_padded, first, 2 * TOK_DEV, 0)
        key_pos = lax.dynamic_slice_in_dim(pos_padded, first, 2 * TOK_DEV, 0)
        query_docs = lax.dynamic_slice_in_dim(docs_padded, own_first, TOK_DEV, 0)
        query_pos = lax.dynamic_slice_in_dim(pos_padded, own_first, TOK_DEV, 0)
        return block_attention(query_rows, key_now, value_now, residual, query_docs, key_docs, query_pos, key_pos, proj_now)
    results = lax.map(one_block, jnp.arange(total_rows // TOK_DEV).astype(jnp.int32))
    return results.reshape(total_rows, middle.shape[1])

def reference(inputs, lengths, order, norm_gain, rate, angle, coef, skip, score_gains, out_proj):
    total_rows = inputs.shape[1]
    positions = jnp.arange(total_rows).astype(jnp.int32)
    finished = []
    for slot_index in range(inputs.shape[0]):
        chosen = order[slot_index]
        current = inputs[chosen]
        doc_ends = jnp.cumsum(lengths[chosen]).astype(jnp.int32)
        doc_ids = lax.optimization_barrier(jnp.sum((doc_ends[None, :] <= positions[:, None]).astype(jnp.int32), axis=1)).astype(jnp.int32)
        for section_index in range(norm_gain.shape[0]):
            tables_all = mode_tables(rate[section_index], angle[section_index], coef[section_index])
            plain = current.astype(jnp.float32)
            scaled = rms_scaled(plain) * norm_gain[section_index]
            mixed = ssm_mix(scaled, doc_ids, tables_all, skip[section_index])
            middle = (plain + mixed).astype(jnp.bfloat16)
            current = doc_attention(middle, doc_ids, score_gains[section_index], out_proj[section_index])
        finished.append(current)
    return jnp.stack(finished)
```

```python
import functools
import itertools

import jax
import jax.numpy as jnp
import numpy as np
from jax import lax
from jax.experimental import pallas as pl
from jax.experimental.pallas import tpu as pltpu
from jax.sharding import PartitionSpec as P

HEAD_DIM = 128
norm_eps = 1e-06
masked_score = -1e30
lanes = 128
mode_group = 4
row_tile = 16


def mixer_tables(rate_now, angle_now, coef_now):
    magnitude = jnp.exp(-rate_now)
    turn_re = magnitude * jnp.cos(angle_now)
    turn_im = magnitude * jnp.sin(angle_now)
    pole_sum = 2.0 * turn_re
    pole_product = -(magnitude * magnitude)
    direct = 2.0 * coef_now[0]
    delayed = -2.0 * (coef_now[0] * turn_re + coef_now[1] * turn_im)
    return jnp.concatenate([pole_sum, pole_product, direct, delayed])


def inverse_rms(values):
    return lax.rsqrt(jnp.mean(values * values, axis=1, keepdims=True) + norm_eps)


def mix_attend_kernel(
    keep_ref, x_ref, table_ref, vec_ref, doc_col_ref, doc_row_ref,
    middle_ref, attended_ref, signal, mixed, queries, keys,
):
    rows, width = x_ref.shape
    folds = width // lanes
    modes = table_ref.shape[0] // 4
    heads = width // HEAD_DIM

    def spread(tile, carry):
        first = pl.multiple_of(tile * row_tile, row_tile)
        plain = x_ref[pl.ds(first, row_tile), :].astype(jnp.float32)
        scaled = plain * inverse_rms(plain) * vec_ref[0:1, :]
        direct = scaled * vec_ref[1:2, :]
        for fold in range(folds):
            where = pl.ds(first * folds + fold, row_tile, stride=folds)
            part = slice(fold * lanes, (fold + 1) * lanes)
            signal[where, :] = scaled[:, part]
            mixed[where, :] = direct[:, part]
        return carry

    lax.fori_loop(0, rows // row_tile, spread, 0)

    def run_modes(group, carry):
        first_mode = group * mode_group

        def table(kind, index):
            return table_ref[kind * modes + first_mode + index]

        coefs = [[table(kind, index) for kind in range(4)] for index in range(mode_group)]

        def advance(chunk, state):
            state = list(state)
            for step in range(8):
                row = chunk * 8 + step
                where = pl.ds(pl.multiple_of(row * folds, folds), folds)
                keep = keep_ref[row]
                entering = signal[where, :]
                total = mixed[where, :]
                for index in range(mode_group):
                    a1, a2, b0, b1 = coefs[index]
                    older = state[2 * index + 1] * keep
                    newer = state[2 * index] * keep
                    now = (entering + a2 * older) + a1 * newer
                    total = total + (b0 * now + b1 * newer)
                    state[2 * index] = now
                    state[2 * index + 1] = newer
                mixed[where, :] = total
            return tuple(state)

        zeros = jnp.zeros((folds, lanes), jnp.float32)
        lax.fori_loop(0, rows // 8, advance, (zeros,) * (2 * mode_group))
        return carry

    lax.fori_loop(0, modes // mode_group, run_modes, 0)

    def gather_back(tile, carry):
        first = pl.multiple_of(tile * row_tile, row_tile)
        where_rows = pl.ds(first, row_tile)
        parts = [
            mixed[pl.ds(first * folds + fold, row_tile, stride=folds), :] for fold in range(folds)
        ]
        plain = x_ref[where_rows, :].astype(jnp.float32)
        middle = (plain + jnp.concatenate(parts, axis=1)).astype(jnp.bfloat16)
        middle_ref[where_rows, :] = middle
        wide = middle.astype(jnp.float32)
        normed = wide * inverse_rms(wide)
        queries[where_rows, :] = (normed * vec_ref[2:3, :]).astype(jnp.bfloat16)
        keys[where_rows, :] = (normed * vec_ref[3:4, :]).astype(jnp.bfloat16)
        return carry

    lax.fori_loop(0, rows // row_tile, gather_back, 0)

    query_pos = lax.broadcasted_iota(jnp.int32, (rows, rows), 0)
    key_pos = lax.broadcasted_iota(jnp.int32, (rows, rows), 1)
    allowed = (key_pos <= query_pos) & (doc_col_ref[...] == doc_row_ref[...])

    def attend(head, carry):
        where = pl.ds(pl.multiple_of(head * HEAD_DIM, HEAD_DIM), HEAD_DIM)
        scores = lax.dot_general(
            queries[:, where], keys[:, where], (((1,), (1,)), ((), ())),
            preferred_element_type=jnp.float32,
        ) * HEAD_DIM ** (-0.5)
        scores = jnp.where(allowed, scores, masked_score)
        raw = jnp.exp(scores - jnp.max(scores, axis=1, keepdims=True))
        weights = (raw * (1.0 / jnp.sum(raw, axis=1, keepdims=True))).astype(jnp.bfloat16)
        attended_ref[:, where] = jnp.dot(
            weights, middle_ref[:, where], preferred_element_type=jnp.float32
        ).astype(jnp.bfloat16)
        return carry

    lax.fori_loop(0, heads, attend, 0)


def mix_attend(x, table, vec, keep, docs):
    rows, width = x.shape
    folds = width // lanes
    vmem = pl.BlockSpec(memory_space=pltpu.VMEM)
    return pl.pallas_call(
        mix_attend_kernel,
        out_shape=[jax.ShapeDtypeStruct((rows, width), jnp.bfloat16)] * 2,
        in_specs=[pl.BlockSpec(memory_space=pltpu.SMEM)] + [vmem] * 5,
        out_specs=[vmem, vmem],
        scratch_shapes=[
            pltpu.VMEM((rows * folds, lanes), jnp.float32),
            pltpu.VMEM((rows * folds, lanes), jnp.float32),
            pltpu.VMEM((rows, width), jnp.bfloat16),
            pltpu.VMEM((rows, width), jnp.bfloat16),
        ],
        compiler_params=pltpu.CompilerParams(vmem_limit_bytes=32 << 20),
        cost_estimate=pl.CostEstimate(
            flops=rows * width * 16 * 10, bytes_accessed=rows * width * 12, transcendentals=0
        ),
        name="mix_attend",
    )(keep, x, table, vec, docs[:, None], docs[None, :])


def permuted_rows(value, order):
    count = lax.axis_size("pipe")
    choices = list(itertools.permutations(range(count)))
    match = jnp.all(jnp.asarray(np.array(choices, np.int32)) == order[None, :], axis=1)
    which = jnp.argmax(match).astype(jnp.int32)

    def mover(choice):
        pairs = [(source, target) for target, source in enumerate(choice)]
        return lambda held: lax.ppermute(held, "pipe", pairs)

    return lax.switch(which, [mover(choice) for choice in choices], value)


def local(inputs, lengths, order, norm_gain, rate, angle, coef, skip, score_gains, out_proj):
    section_count = lax.axis_size("pipe")
    seq_count = lax.axis_size("seq")
    pipe_index = lax.axis_index("pipe")
    seq_index = lax.axis_index("seq")
    row_count, width = inputs.shape[1:]
    shard = out_proj.shape[1]

    quarters = lax.all_to_all(
        out_proj[0].reshape(section_count, shard // section_count, width),
        "pipe", split_axis=0, concat_axis=0, tiled=True,
    )
    projections = [
        lax.all_gather(quarters[section], ("seq", "pipe"), axis=0, tiled=True)
        for section in range(section_count)
    ]

    table_own = mixer_tables(rate[0], angle[0], coef[0]).reshape(-1, width // lanes, lanes)
    vec_own = jnp.concatenate([norm_gain, skip, score_gains[0]])
    tables = lax.all_gather(table_own, "pipe")
    vecs = lax.all_gather(vec_own, "pipe")

    own = permuted_rows(inputs[0], order)
    before = lax.ppermute(own, "seq", [(i, i + 1) for i in range(seq_count - 1)])
    x = jnp.concatenate([before, own])

    positions = (seq_index - 1) * row_count + jnp.arange(2 * row_count)
    chosen = lax.dynamic_index_in_dim(order, pipe_index, 0, False)
    doc_ends = jnp.cumsum(lax.dynamic_index_in_dim(lengths, chosen, 0, False))
    counted = jnp.sum((doc_ends[None, :] <= positions[:, None]).astype(jnp.int32), axis=1)
    docs = jnp.where(positions >= 0, counted, -1)
    keep = jnp.concatenate([jnp.zeros((1,), jnp.float32), (docs[1:] == docs[:-1]).astype(jnp.float32)])

    for section in range(section_count):
        middle, attended = mix_attend(x, tables[section], vecs[section], keep, docs)
        if section == section_count - 1:
            middle = middle[row_count:]
            attended = attended[row_count:]
        projected = jnp.dot(attended, projections[section], preferred_element_type=jnp.float32)
        x = (middle.astype(jnp.float32) + projected).astype(jnp.bfloat16)
    return x[None]


def solution(mesh):
    in_specs = (
        P("pipe", "seq", None),
        P(),
        P(),
        P("pipe", None),
        P("pipe", None, None),
        P("pipe", None, None),
        P("pipe", None, None, None),
        P("pipe", None),
        P("pipe", None, None),
        P("pipe", "seq", None),
    )
    out_specs = P("pipe", "seq", None)
    return jax.shard_map(local, mesh=mesh, in_specs=in_specs, out_specs=out_specs, check_vma=False)
```

```python
import functools
import itertools
import math

import jax
import jax.numpy as jnp
import numpy as np
from jax import lax
from jax.experimental import pallas as pl
from jax.experimental.pallas import tpu as pltpu
from jax.sharding import PartitionSpec as P

HEAD_DIM = 128
norm_eps = 1e-06
masked_score = -1e30
lanes = 128
mode_group = 4
chunk_rows = 8
vector_rows = 4
row_tile = 16


def mixer_tables(rate_now, angle_now, coef_now, skip_now, vectors):
    magnitude = jnp.exp(-rate_now)
    turn_re = magnitude * jnp.cos(angle_now)
    turn_im = magnitude * jnp.sin(angle_now)
    pole_sum = 2.0 * turn_re
    pole_product = -(magnitude * magnitude)
    direct = 2.0 * coef_now[0]
    delayed = -2.0 * (coef_now[0] * turn_re + coef_now[1] * turn_im)
    through = jnp.broadcast_to(skip_now, vectors.shape)
    halves = jnp.stack([
        jnp.concatenate([pole_sum, pole_product, through]),
        jnp.concatenate([direct, delayed, vectors]),
    ])
    return halves.reshape(halves.shape[:2] + (-1, lanes))


def inverse_rms(values):
    return lax.rsqrt(jnp.mean(values * values, axis=1, keepdims=True) + norm_eps)


def mix_attend_kernel(
    keep_ref, broken_ref, x_ref, pole_ref, zero_ref, vec_ref, doc_col_ref, doc_row_ref,
    middle_ref, attended_ref, signal, mixed, queries, keys,
):
    rows, width = x_ref.shape
    own = rows // 2
    folds = width // lanes
    modes = (pole_ref.shape[0] - vec_ref.shape[0]) // 2
    heads = width // HEAD_DIM

    def spread(tile, carry):
        first = pl.multiple_of(tile * row_tile, row_tile)
        plain = x_ref[pl.ds(first, row_tile), :].astype(jnp.float32)
        scaled = plain * inverse_rms(plain) * vec_ref[0:1, :]
        for fold in range(folds):
            where = pl.ds(first * folds + fold, row_tile, stride=folds)
            signal[where, :] = scaled[:, fold * lanes : (fold + 1) * lanes]
        return carry

    lax.fori_loop(0, rows // row_tile, spread, 0, unroll=2)

    first_chunk = broken_ref[rows // chunk_rows]

    def run_modes(group, opening):
        first_mode = group * mode_group
        coefs = [
            [
                ref[kind * modes + first_mode + index]
                for ref in (pole_ref, zero_ref)
                for kind in range(2)
            ]
            for index in range(mode_group)
        ]
        through = pole_ref[2 * modes] if opening else None

        def advance(chunk, state):
            def steps(state, masked):
                state = list(state)
                for step in range(chunk_rows):
                    row = chunk * chunk_rows + step
                    where = pl.ds(pl.multiple_of(row * folds, folds), folds)
                    entering = signal[where, :]
                    total = through * entering if opening else mixed[where, :]
                    for index in range(mode_group):
                        a1, a2, b0, b1 = coefs[index]
                        newer, older = state[2 * index], state[2 * index + 1]
                        if masked:
                            keep = keep_ref[row]
                            newer, older = newer * keep, older * keep
                        now = (entering + a2 * older) + a1 * newer
                        total = total + (b0 * now + b1 * newer)
                        state[2 * index], state[2 * index + 1] = now, newer
                    mixed[where, :] = total
                return tuple(state)

            return lax.cond(
                broken_ref[chunk] > 0,
                lambda held: steps(held, True),
                lambda held: steps(held, False),
                state,
            )

        zeros = jnp.zeros((folds, lanes), jnp.float32)
        lax.fori_loop(first_chunk, rows // chunk_rows, advance, (zeros,) * (2 * mode_group))

    run_modes(0, True)

    def later_modes(group, carry):
        run_modes(group, False)
        return carry

    lax.fori_loop(1, modes // mode_group, later_modes, 0)

    def gather_back(tile, carry):
        first = pl.multiple_of(tile * row_tile, row_tile)
        where_rows = pl.ds(first, row_tile)
        parts = [
            mixed[pl.ds(first * folds + fold, row_tile, stride=folds), :] for fold in range(folds)
        ]
        plain = x_ref[where_rows, :].astype(jnp.float32)
        middle = (plain + jnp.concatenate(parts, axis=1)).astype(jnp.bfloat16)
        middle_ref[where_rows, :] = middle
        wide = middle.astype(jnp.float32)
        normed = wide * inverse_rms(wide)
        queries[where_rows, :] = (normed * vec_ref[1:2, :]).astype(jnp.bfloat16)
        keys[where_rows, :] = (normed * vec_ref[2:3, :]).astype(jnp.bfloat16)
        return carry

    def clear(tile, carry):
        first = pl.multiple_of(tile * row_tile, row_tile)
        middle_ref[pl.ds(first, row_tile), :] = jnp.zeros((row_tile, width), jnp.bfloat16)
        queries[pl.ds(first, row_tile), :] = jnp.zeros((row_tile, width), jnp.bfloat16)
        keys[pl.ds(first, row_tile), :] = jnp.zeros((row_tile, width), jnp.bfloat16)
        return carry

    first_tile = first_chunk // (row_tile // chunk_rows)
    lax.fori_loop(0, first_tile, clear, 0)
    lax.fori_loop(first_tile, rows // row_tile, gather_back, 0)

    query_pos = lax.broadcasted_iota(jnp.int32, (own, rows), 0) + own
    key_pos = lax.broadcasted_iota(jnp.int32, (own, rows), 1)
    allowed_own = (key_pos <= query_pos) & (doc_col_ref[own:, :] == doc_row_ref[...])
    allowed_halo = (key_pos[:, :own] <= query_pos[:, :own] - own) & (
        doc_col_ref[:own, :] == doc_row_ref[:, :own]
    )
    rate = HEAD_DIM ** (-0.5) * math.log2(math.e)

    def attend(head, carry):
        where = pl.ds(pl.multiple_of(head * HEAD_DIM, HEAD_DIM), HEAD_DIM)
        for first, count, allowed in ((0, own, allowed_halo), (own, rows, allowed_own)):
            scores = lax.dot_general(
                queries[first : first + own, where], keys[:count, where], (((1,), (1,)), ((), ())),
                preferred_element_type=jnp.float32,
            )
            scores = jnp.where(allowed, scores, masked_score)
            raw = jnp.exp2((scores - jnp.max(scores, axis=1, keepdims=True)) * rate)
            weights = (raw * (1.0 / jnp.sum(raw, axis=1, keepdims=True))).astype(jnp.bfloat16)
            attended_ref[first : first + own, where] = jnp.dot(
                weights, middle_ref[:count, where], preferred_element_type=jnp.float32
            ).astype(jnp.bfloat16)
        return carry

    lax.fori_loop(0, heads, attend, 0, unroll=8)


def document_flags(docs):
    goes_on = jnp.concatenate([jnp.zeros((1,), bool), docs[1:] == docs[:-1]])
    broken = jnp.any(jnp.logical_not(goes_on).reshape(-1, chunk_rows), axis=1)
    needed = docs == docs[docs.shape[0] // 2]
    first_chunk = jnp.argmax(needed) // chunk_rows
    flags = jnp.concatenate([broken.astype(jnp.int32), first_chunk.astype(jnp.int32)[None]])
    return goes_on.astype(jnp.float32), flags


def mix_attend(x, poles, zeros, docs, keep, flags):
    rows, width = x.shape
    vec = zeros[-vector_rows:].reshape(vector_rows, width)
    folds = width // lanes
    smem = pl.BlockSpec(memory_space=pltpu.SMEM)
    vmem = pl.BlockSpec(memory_space=pltpu.VMEM)
    return pl.pallas_call(
        mix_attend_kernel,
        out_shape=[jax.ShapeDtypeStruct((rows, width), jnp.bfloat16)] * 2,
        in_specs=[smem, smem] + [vmem] * 6,
        out_specs=[vmem, vmem],
        scratch_shapes=[
            pltpu.VMEM((rows * folds, lanes), jnp.float32),
            pltpu.VMEM((rows * folds, lanes), jnp.float32),
            pltpu.VMEM((rows, width), jnp.bfloat16),
            pltpu.VMEM((rows, width), jnp.bfloat16),
        ],
        compiler_params=pltpu.CompilerParams(vmem_limit_bytes=32 << 20),
        cost_estimate=pl.CostEstimate(
            flops=rows * width * 16 * 10, bytes_accessed=rows * width * 12, transcendentals=0
        ),
        name="mix_attend",
    )(keep, flags, x, poles, zeros, vec, docs[:, None], docs[None, :])


def project_kernel(place_ref, middle_ref, attended_ref, *refs):
    pieces, (out_ref, wholes, halves, arrived) = refs[:5], refs[5:]
    depth, quarter = wholes.shape[1:]
    half = depth // 2
    pipe, core = place_ref[0], place_ref[1]
    targets = [wholes.at[index] for index in range(3)] + [halves.at[index] for index in range(2)]
    copies = [
        pltpu.make_async_copy(piece, target, arrived.at[index])
        for index, (piece, target) in enumerate(zip(pieces, targets))
    ]
    for copy in copies:
        copy.start()

    def times(rows, weights):
        return jnp.dot(rows, weights, preferred_element_type=jnp.float32)

    def columns(first):
        return attended_ref[:, pl.ds(pl.multiple_of(first, 128), half)]

    def finish(hops, total):
        where = pl.ds(pl.multiple_of((pipe ^ hops) * quarter, 128), quarter)
        out_ref[:, where] = (middle_ref[:, where].astype(jnp.float32) + total).astype(jnp.bfloat16)

    for index, hops in enumerate((0, 1 + core, 2 - core)):
        copies[index].wait()
        finish(hops, times(attended_ref[...], wholes[index]))
    copies[3].wait()
    total = times(columns(core * half), halves[0])
    copies[4].wait()
    finish(3, total + times(columns((1 - core) * half), halves[1]))


def project(middle, attended, pieces, place):
    rows, width = middle.shape
    vmem = pl.BlockSpec(memory_space=pltpu.VMEM)
    return pl.pallas_call(
        project_kernel,
        out_shape=jax.ShapeDtypeStruct((rows, width), jnp.bfloat16),
        in_specs=[pl.BlockSpec(memory_space=pltpu.SMEM), vmem, vmem]
        + [pl.BlockSpec(memory_space=pl.ANY)] * len(pieces),
        out_specs=vmem,
        scratch_shapes=[
            pltpu.VMEM((3,) + pieces[0].shape, jnp.bfloat16),
            pltpu.VMEM((2,) + pieces[-1].shape, jnp.bfloat16),
            pltpu.SemaphoreType.DMA((len(pieces),)),
        ],
        compiler_params=pltpu.CompilerParams(vmem_limit_bytes=32 << 20),
        cost_estimate=pl.CostEstimate(
            flops=2 * rows * width * width, bytes_accessed=2 * width * width + 6 * rows * width,
            transcendentals=0,
        ),
        name="project",
    )(place, middle, attended, *pieces)


def across(value, hops):
    count = lax.axis_size("pipe")
    return lax.ppermute(value, "pipe", [(i, i ^ hops) for i in range(count)])


def swapped(value):
    count = lax.axis_size("seq")
    return lax.ppermute(value, "seq", [(i, i ^ 1) for i in range(count)])


def spread_quarters(shard):
    section_count = lax.axis_size("pipe")
    pipe_index = lax.axis_index("pipe")
    quarter = shard.shape[1] // section_count

    def columns(index):
        return lax.dynamic_slice_in_dim(shard, index * quarter, quarter, 1)

    spread = [columns(pipe_index)]
    spread += [across(columns(pipe_index ^ hops), hops) for hops in range(1, section_count)]
    spread = jnp.stack(spread)
    return [
        lax.dynamic_index_in_dim(spread, pipe_index ^ section, 0, False)
        for section in range(section_count)
    ]


def spread_tables(halves):
    section_count = lax.axis_size("pipe")
    pipe_index = lax.axis_index("pipe")
    core = lax.axis_index("seq") % 2
    mine = lax.dynamic_index_in_dim(halves, core, 0, False)
    fetched = jnp.stack([across(mine, hops) for hops in range(1, section_count)])
    other = swapped(fetched)
    own = jnp.where(core == 0, halves, halves[::-1])
    held = jnp.concatenate([own, jnp.stack([fetched, other], axis=1).reshape((-1,) + mine.shape)])
    return [
        [
            lax.dynamic_index_in_dim(held, 2 * (pipe_index ^ section) + which, 0, False)
            for which in (core, 1 - core)
        ]
        for section in range(section_count)
    ]


def sent_by_core(value, hops_by_core):
    pipe_count, seq_count = lax.axis_size("pipe"), lax.axis_size("seq")
    pairs = [
        (pipe * seq_count + seq, (pipe ^ hops_by_core[seq % 2]) * seq_count + seq)
        for pipe in range(pipe_count)
        for seq in range(seq_count)
    ]
    return lax.ppermute(value, ("pipe", "seq"), pairs)


def passed_on(fetched):
    half = fetched.shape[0] // 2
    core = lax.axis_index("seq") % 2
    return sent_by_core(lax.dynamic_slice_in_dim(fetched, core * half, half, 0), (2, 1))


def permuted_rows(value, order):
    count = lax.axis_size("pipe")
    choices = list(itertools.permutations(range(count)))
    match = jnp.all(jnp.asarray(np.array(choices, np.int32)) == order[None, :], axis=1)
    which = jnp.argmax(match).astype(jnp.int32)

    def mover(choice):
        pairs = [(source, target) for target, source in enumerate(choice)]
        return lambda held: lax.ppermute(held, "pipe", pairs)

    return lax.switch(which, [mover(choice) for choice in choices], value)


def local(inputs, lengths, order, norm_gain, rate, angle, coef, skip, score_gains, out_proj):
    section_count = lax.axis_size("pipe")
    seq_count = lax.axis_size("seq")
    pipe_index = lax.axis_index("pipe")
    seq_index = lax.axis_index("seq")
    row_count = inputs.shape[1]

    place = jnp.stack([pipe_index, seq_index % 2]).astype(jnp.int32)
    vectors = jnp.concatenate([norm_gain, score_gains[0], skip])
    halves = mixer_tables(rate[0], angle[0], coef[0], skip[0], vectors)

    quarters = spread_quarters(out_proj[0])
    quarters, halves, entering = lax.optimization_barrier((quarters, halves, inputs[0]))
    wholes = [lax.all_gather(quarter, "seq", axis=0, tiled=True) for quarter in quarters]

    own = permuted_rows(entering, order)
    before = lax.ppermute(own, "seq", [(i, i + 1) for i in range(seq_count - 1)])
    x = jnp.concatenate([before, own])
    tables = spread_tables(halves)

    positions = (seq_index - 1) * row_count + jnp.arange(2 * row_count)
    chosen = lax.dynamic_index_in_dim(order, pipe_index, 0, False)
    doc_ends = jnp.cumsum(lax.dynamic_index_in_dim(lengths, chosen, 0, False))
    counted = jnp.sum((doc_ends[None, :] <= positions[:, None]).astype(jnp.int32), axis=1)
    docs = jnp.where(positions >= 0, counted, -1)
    keep, flags = document_flags(docs)

    def hop(section):
        return sent_by_core(wholes[section], (1, 2))

    def mix(section, x):
        return mix_attend(x, *tables[section], docs, keep, flags)

    def weights(section):
        return [
            wholes[section], near[section], swapped(near[section]),
            far[section], swapped(far[section]),
        ]

    tie = lax.optimization_barrier
    near, far = {}, {}
    x, tables[0], wholes[0] = tie((x, tables[0], wholes[0]))
    near[0] = hop(0)
    middle, attended = mix(0, x)
    near[0], middle, attended, wholes[1] = tie((near[0], middle, attended, wholes[1]))
    far[0] = passed_on(near[0])
    near[1] = hop(1)
    far[0], wholes[2] = tie((far[0], wholes[2]))
    pieces = weights(0)
    near[2] = hop(2)
    near[1], wholes[2], middle, attended = tie((near[1], wholes[2], middle, attended))
    far[1] = passed_on(near[1])
    x = project(middle, attended, pieces, place)
    middle, attended = mix(1, x)
    middle, attended, wholes[3] = tie((middle, attended, wholes[3]))
    near[3] = hop(3)
    for section in range(1, section_count):
        last = section == section_count - 1
        if last:
            far[section], middle, attended = tie((far[section], middle, attended))
            x = project(middle[row_count:], attended[row_count:], weights(section), place)
        else:
            held = (far[section], near[section + 1], middle, attended)
            far[section], near[section + 1], middle, attended = tie(held)
            far[section + 1] = passed_on(near[section + 1])
            x = project(middle, attended, weights(section), place)
            middle, attended = mix(section + 1, x)
    return x[None]


def solution(mesh):
    in_specs = (
        P("pipe", "seq", None),
        P(),
        P(),
        P("pipe", None),
        P("pipe", None, None),
        P("pipe", None, None),
        P("pipe", None, None, None),
        P("pipe", None),
        P("pipe", None, None),
        P("pipe", "seq", None),
    )
    out_specs = P("pipe", "seq", None)
    return jax.shard_map(local, mesh=mesh, in_specs=in_specs, out_specs=out_specs, check_vma=False)
```

```python
import functools
import itertools
import math

import jax
import jax.numpy as jnp
import numpy as np
from jax import lax
from jax.experimental import pallas as pl
from jax.experimental.pallas import tpu as pltpu
from jax.sharding import PartitionSpec as P

HEAD_DIM = 128
norm_eps = 1e-06
masked_score = -1e30
lanes = 128
mode_group = 8
chunk_rows = 16
seq_far = 2
head_batch = 8
vector_rows = 4
row_tile = 16


def mixer_tables(rate_now, angle_now, coef_now, skip_now, vectors):
    magnitude = jnp.exp(-rate_now)
    turn_re = magnitude * jnp.cos(angle_now)
    turn_im = magnitude * jnp.sin(angle_now)
    pole_sum = 2.0 * turn_re
    pole_product = -(magnitude * magnitude)
    direct = 2.0 * coef_now[0]
    delayed = -2.0 * (coef_now[0] * turn_re + coef_now[1] * turn_im)
    through = jnp.broadcast_to(skip_now, vectors.shape)
    halves = jnp.stack([
        jnp.concatenate([pole_sum, pole_product, through]),
        jnp.concatenate([direct, delayed, vectors]),
    ])
    return halves.reshape(halves.shape[:2] + (-1, lanes))


def inverse_rms(values):
    return lax.rsqrt(jnp.mean(values * values, axis=1, keepdims=True) + norm_eps)


def fetch(sources, targets, arrived):
    copies = [
        pltpu.make_async_copy(source, target, arrived.at[index])
        for index, (source, target) in enumerate(zip(sources, targets))
    ]
    for copy in copies:
        copy.start()
    return copies


def times(rows, weights):
    return jnp.dot(rows, weights, preferred_element_type=jnp.float32)


def add_projection(place_ref, out_ref, middle_ref, attended_ref, wholes, halves, copies):
    pipe, core = place_ref[0], place_ref[1]
    quarter = wholes.shape[2]

    def put(index, total):
        where = pl.ds(pl.multiple_of(index * quarter, lanes), quarter)
        out_ref[:, where] = (middle_ref[:, where].astype(jnp.float32) + total).astype(jnp.bfloat16)

    for index, hops in zip(range(wholes.shape[0]), (0, 1 + core, 2 - core, 3)):
        copies[index].wait()
        put(pipe ^ hops, times(attended_ref[...], wholes[index]))
    if halves is None:
        return
    half = halves.shape[1]
    total = 0.0
    for index, first in enumerate((core * half, (1 - core) * half)):
        copies[3 + index].wait()
        rows = attended_ref[:, pl.ds(pl.multiple_of(first, lanes), half)]
        total = total + times(rows, halves[index])
    put(pipe ^ 3, total)


def mix_attend(
    keep_ref, broken_ref, doc_col_ref, doc_row_ref, x_ref, pole_ref, zero_ref, middle_ref,
    attended_refs, signal, mixed, queries, keys, with_halo, after_middle, after_half,
):
    rows, width = x_ref.shape
    own = rows // 2
    folds = width // lanes
    modes = (pole_ref.shape[0] - vector_rows) // 2
    heads = width // HEAD_DIM
    tiles = rows // row_tile
    first_chunk = broken_ref[rows // chunk_rows]
    first_tile = first_chunk // (2 * row_tile // chunk_rows) * 2

    def gain(row, fold):
        return zero_ref[2 * modes + row, fold : fold + 1, :]

    def in_pairs(body, first, last):
        def pair(index, carry):
            return body(2 * index + 1, body(2 * index, carry))

        lax.fori_loop(first // 2, last // 2, pair, 0)

    def spread(tile, carry):
        first = pl.multiple_of(tile * row_tile, row_tile)
        plain = x_ref[pl.ds(first, row_tile), :].astype(jnp.float32)
        scaled = plain * inverse_rms(plain)
        for fold in range(folds):
            where = pl.ds(first * folds + fold, row_tile, stride=folds)
            signal[where, :] = scaled[:, fold * lanes : (fold + 1) * lanes] * gain(0, fold)
        return carry

    in_pairs(spread, first_tile, tiles)

    def run_modes(group, opening):
        first_mode = group * mode_group
        coefs = [
            [
                ref[kind * modes + first_mode + index]
                for ref in (pole_ref, zero_ref)
                for kind in range(2)
            ]
            for index in range(mode_group)
        ]
        through = pole_ref[2 * modes] if opening else None

        def advance(chunk, state):
            def steps(state, masked):
                state = list(state)
                for step in range(chunk_rows):
                    row = chunk * chunk_rows + step
                    where = pl.ds(pl.multiple_of(row * folds, folds), folds)
                    entering = signal[where, :]
                    total = through * entering if opening else mixed[where, :]
                    for index in range(mode_group):
                        a1, a2, b0, b1 = coefs[index]
                        newer, older = state[2 * index], state[2 * index + 1]
                        if masked:
                            keep = keep_ref[row]
                            newer, older = newer * keep, older * keep
                        now = (entering + a2 * older) + a1 * newer
                        total = total + (b0 * now + b1 * newer)
                        state[2 * index], state[2 * index + 1] = now, newer
                    mixed[where, :] = total
                return tuple(state)

            return lax.cond(
                broken_ref[chunk] > 0,
                lambda held: steps(held, True),
                lambda held: steps(held, False),
                state,
            )

        zeros = jnp.zeros((folds, lanes), jnp.float32)
        lax.fori_loop(first_chunk, rows // chunk_rows, advance, (zeros,) * (2 * mode_group))

    run_modes(0, True)

    def later_modes(group, carry):
        run_modes(group, False)
        return carry

    lax.fori_loop(1, modes // mode_group, later_modes, 0)

    def gather_back(tile, carry):
        first = pl.multiple_of(tile * row_tile, row_tile)
        where_rows = pl.ds(first, row_tile)
        parts = [
            mixed[pl.ds(first * folds + fold, row_tile, stride=folds), :] for fold in range(folds)
        ]
        plain = x_ref[where_rows, :].astype(jnp.float32)
        middle = (plain + jnp.concatenate(parts, axis=1)).astype(jnp.bfloat16)
        middle_ref[where_rows, :] = middle
        wide = middle.astype(jnp.float32)
        normed = wide * inverse_rms(wide)
        for fold in range(folds):
            part = slice(fold * lanes, (fold + 1) * lanes)
            queries[where_rows, part] = (normed[:, part] * gain(1, fold)).astype(jnp.bfloat16)
            keys[where_rows, part] = (normed[:, part] * gain(2, fold)).astype(jnp.bfloat16)
        return carry

    def clear(tile, carry):
        first = pl.multiple_of(tile * row_tile, row_tile)
        for ref in (middle_ref, queries, keys):
            ref[pl.ds(first, row_tile), :] = jnp.zeros((row_tile, width), jnp.bfloat16)
        return carry

    in_pairs(clear, 0, first_tile)
    in_pairs(gather_back, first_tile, tiles)
    after_middle()

    query_pos = lax.broadcasted_iota(jnp.int32, (own, rows), 0) + own
    key_pos = lax.broadcasted_iota(jnp.int32, (own, rows), 1)
    allowed_own = (key_pos <= query_pos) & (doc_col_ref[own:, :] == doc_row_ref[...])
    allowed_halo = (key_pos[:, :own] <= query_pos[:, :own] - own) & (
        doc_col_ref[:own, :] == doc_row_ref[:, :own]
    )
    rate = HEAD_DIM ** (-0.5) * math.log2(math.e)
    blocks = [(own, rows, allowed_own)]
    if with_halo:
        blocks.insert(0, (0, own, allowed_halo))
    skipped = rows - own * len(blocks)
    for batch in range(0, heads, head_batch):
        jobs = [
            (head, first, count, allowed)
            for head in range(batch, batch + head_batch)
            for first, count, allowed in blocks
        ]
        raws = []
        for head, first, count, allowed in jobs:
            where = slice(head * HEAD_DIM, (head + 1) * HEAD_DIM)
            scores = lax.dot_general(
                queries[first : first + own, where], keys[:count, where], (((1,), (1,)), ((), ())),
                preferred_element_type=jnp.float32,
            )
            raws.append(jnp.where(allowed, scores, masked_score))
        tops = [jnp.max(raw, axis=1, keepdims=True) for raw in raws]
        raws = [jnp.exp2((raw - top) * rate) for raw, top in zip(raws, tops)]
        sums = [jnp.sum(raw, axis=1, keepdims=True) for raw in raws]
        raws = [(raw * (1.0 / total)).astype(jnp.bfloat16) for raw, total in zip(raws, sums)]
        for (head, first, count, _), weights in zip(jobs, raws):
            where = slice(head * HEAD_DIM, (head + 1) * HEAD_DIM)
            part, inner = divmod(head, heads // 2)
            placed = slice(inner * HEAD_DIM, (inner + 1) * HEAD_DIM)
            attended_refs[part][first - skipped : first - skipped + own, placed] = times(
                weights, middle_ref[:count, where]
            ).astype(jnp.bfloat16)
        if (batch + head_batch) % (heads // 2) == 0:
            after_half(batch // (heads // 2))


def section_kernel(wholes_count, halves_count, mixes, with_halo, *refs):
    refs = list(refs)

    def take(count):
        taken, refs[:count] = refs[:count], []
        return taken

    place_ref, = take(1)
    if mixes:
        keep_ref, broken_ref, doc_col_ref, doc_row_ref, tables_ref = take(5)
    sources, weights = take(2), take(wholes_count + halves_count)
    if mixes:
        middle_out, attended_out = take(2)
    else:
        out_ref, = take(1)
    arrived, = take(1)
    if mixes:
        x_ref, pole_ref, zero_ref, middle_ref, low_ref, high_ref, signal, mixed, queries, keys = take(10)
        copies = fetch(
            [tables_ref.at[place_ref[2]], tables_ref.at[place_ref[3]]], [pole_ref, zero_ref],
            arrived.at[pl.ds(10, 2)],
        )
    if weights:
        middle_in, attended_in, wholes = take(3)
        halves = take(1)[0] if halves_count else None
        skipped = sources[0].shape[0] - middle_in.shape[0]
        rows = pl.ds(skipped, middle_in.shape[0])
        inputs = fetch([source.at[rows] for source in sources], [middle_in, attended_in], arrived)
        targets = [wholes.at[index] for index in range(wholes_count)]
        targets += [halves.at[index] for index in range(halves_count)]
        pieces = fetch(weights, targets, arrived.at[pl.ds(2, 5)])
        for copy in inputs:
            copy.wait()
        target = x_ref if mixes else out_ref
        add_projection(place_ref, target, middle_in, attended_in, wholes, halves, pieces)
    else:
        own = x_ref.shape[0] // 2
        inputs = fetch(sources, [x_ref.at[pl.ds(0, own)], x_ref.at[pl.ds(own, own)]], arrived)
        for copy in inputs:
            copy.wait()
    if not mixes:
        return
    for copy in copies:
        copy.wait()
    skipped = middle_ref.shape[0] - middle_out.shape[0]
    half = low_ref.shape[1]
    results = [
        pltpu.make_async_copy(
            middle_ref.at[pl.ds(skipped, middle_out.shape[0])], middle_out, arrived.at[7]
        )
    ] + [
        pltpu.make_async_copy(
            ref, attended_out.at[:, pl.ds(index * half, half)], arrived.at[8 + index]
        )
        for index, ref in enumerate((low_ref, high_ref))
    ]
    mix_attend(
        keep_ref, broken_ref, doc_col_ref, doc_row_ref, x_ref, pole_ref, zero_ref, middle_ref,
        (low_ref, high_ref), signal, mixed, queries, keys, with_halo,
        results[0].start, lambda part: results[1 + part].start(),
    )
    for copy in results:
        copy.wait()


def section_step(place, sources, weights=(), mixing=(), with_halo=True):
    width = sources[0].shape[1]
    smem, vmem, anywhere = (
        pl.BlockSpec(memory_space=space) for space in (pltpu.SMEM, pltpu.VMEM, pltpu.HBM)
    )
    rows = sources[0].shape[0] if weights else 2 * sources[0].shape[0]
    folds = width // lanes
    wholes_count = sum(weight.shape[0] == width for weight in weights)
    halves_count = len(weights) - wholes_count
    scratch = [pltpu.SemaphoreType.DMA((12,))]
    if mixing:
        kept = rows if with_halo else rows // 2
        wide = pltpu.VMEM((rows * folds, lanes), jnp.float32)
        narrow = pltpu.VMEM((rows, width), jnp.bfloat16)
        half = pltpu.VMEM((kept, width // 2), jnp.bfloat16)
        table = pltpu.VMEM(mixing[-1].shape[1:], jnp.float32)
        scratch += [narrow, table, table, narrow, half, half, wide, wide, narrow, narrow]
        out_shape = [jax.ShapeDtypeStruct((kept, width), jnp.bfloat16)] * 2
        out_specs = [anywhere, anywhere]
    else:
        kept = rows
        out_shape = jax.ShapeDtypeStruct((rows, width), jnp.bfloat16)
        out_specs = vmem
    if weights:
        held = pltpu.VMEM((rows, width), jnp.bfloat16)
        scratch += [
            held, held,
            pltpu.VMEM((wholes_count,) + weights[0].shape, jnp.bfloat16),
        ]
        if halves_count:
            scratch.append(pltpu.VMEM((halves_count,) + weights[-1].shape, jnp.bfloat16))
    return pl.pallas_call(
        functools.partial(section_kernel, wholes_count, halves_count, bool(mixing), with_halo),
        out_shape=out_shape,
        in_specs=[smem]
        + ([smem, smem, vmem, vmem, anywhere] if mixing else [])
        + [anywhere] * (len(sources) + len(weights)),
        out_specs=out_specs,
        scratch_shapes=scratch,
        compiler_params=pltpu.CompilerParams(vmem_limit_bytes=60 << 20),
        cost_estimate=pl.CostEstimate(
            flops=2 * rows * width * width, bytes_accessed=2 * width * width, transcendentals=0
        ),
        name="section_step",
    )(place, *mixing, *sources, *weights)


def half_copy_kernel(place_ref, value_ref, out_ref, held, arrived, left):
    half = out_ref.shape[0]
    part = half // 4
    parts = [pl.ds(index * part, part) for index in range(4)]
    starts = [place_ref[1] * half + index * part for index in range(4)]
    sources = [value_ref.at[pl.ds(first, part)] for first in starts]
    coming = fetch(sources, [held.at[where] for where in parts], arrived)
    going = []
    for index, where in enumerate(parts):
        coming[index].wait()
        going.append(pltpu.make_async_copy(held.at[where], out_ref.at[where], left.at[index]))
        going[-1].start()
    for copy in going:
        copy.wait()


def core_half(value, place):
    hbm = pl.BlockSpec(memory_space=pltpu.HBM)
    shape = (value.shape[0] // 2,) + value.shape[1:]
    return pl.pallas_call(
        half_copy_kernel,
        out_shape=jax.ShapeDtypeStruct(shape, value.dtype),
        in_specs=[pl.BlockSpec(memory_space=pltpu.SMEM), hbm],
        out_specs=hbm,
        scratch_shapes=[pltpu.VMEM(shape, value.dtype)] + [pltpu.SemaphoreType.DMA((4,))] * 2,
        compiler_params=pltpu.CompilerParams(vmem_limit_bytes=60 << 20),
        name="core_half",
    )(place, value)


def document_flags(docs):
    goes_on = jnp.concatenate([jnp.zeros((1,), bool), docs[1:] == docs[:-1]])
    broken = jnp.any(jnp.logical_not(goes_on).reshape(-1, chunk_rows), axis=1)
    needed = docs == docs[docs.shape[0] // 2]
    first_chunk = jnp.argmax(needed) // chunk_rows
    flags = jnp.concatenate([broken.astype(jnp.int32), first_chunk.astype(jnp.int32)[None]])
    return goes_on.astype(jnp.float32), flags


def across(value, hops):
    count = lax.axis_size("pipe")
    return lax.ppermute(value, "pipe", [(i, i ^ hops) for i in range(count)])


def swapped(value):
    count = lax.axis_size("seq")
    return lax.ppermute(value, "seq", [(i, i ^ 1) for i in range(count)])


def spread_quarters(shard, offset, first):
    section_count = lax.axis_size("pipe")
    pipe_index = lax.axis_index("pipe")
    quarter = shard.shape[1] // section_count

    def columns(hops):
        return lax.dynamic_slice_in_dim(shard, (pipe_index ^ hops ^ offset) * quarter, quarter, 1)

    held = [columns(0)]
    for hops in range(1, section_count):
        pairs = [(i, i ^ hops) for i in range(first, section_count)]
        held.append(lax.ppermute(columns(hops), "pipe", pairs))
    held = jnp.stack(held)
    return {
        section: lax.dynamic_index_in_dim(held, pipe_index ^ section, 0, False)
        for section in range(first, section_count)
    }


def own_half(halves):
    return lax.dynamic_index_in_dim(halves, lax.axis_index("seq") % 2, 0, False)


def joined_tables(halves, fetched):
    fetched = jnp.stack(fetched)
    other = swapped(fetched)
    own = jnp.where(lax.axis_index("seq") % 2 == 0, halves, halves[::-1])
    return jnp.concatenate([own, jnp.stack([fetched, other], axis=1).reshape((-1,) + own.shape[1:])])


def sent_by_core(value, hops_by_core):
    pipe_count, seq_count = lax.axis_size("pipe"), lax.axis_size("seq")
    pairs = [
        (pipe * seq_count + seq, (pipe ^ hops_by_core[seq % 2]) * seq_count + seq)
        for pipe in range(pipe_count)
        for seq in range(seq_count)
    ]
    return lax.ppermute(value, ("pipe", "seq"), pairs)


def passed_on(fetched, place):
    return sent_by_core(core_half(fetched, place), (2, 1))


def permuted_rows(value, order):
    count = lax.axis_size("pipe")
    choices = list(itertools.permutations(range(count)))
    match = jnp.all(jnp.asarray(np.array(choices, np.int32)) == order[None, :], axis=1)
    which = jnp.argmax(match).astype(jnp.int32)

    def mover(choice):
        pairs = [(source, target) for target, source in enumerate(choice)]
        return lambda held: lax.ppermute(held, "pipe", pairs)

    return lax.switch(which, [mover(choice) for choice in choices], value)


def local(inputs, lengths, order, norm_gain, rate, angle, coef, skip, score_gains, out_proj):
    section_count = lax.axis_size("pipe")
    seq_count = lax.axis_size("seq")
    pipe_index = lax.axis_index("pipe")
    seq_index = lax.axis_index("seq")
    row_count = inputs.shape[1]

    place = jnp.stack([pipe_index, seq_index % 2]).astype(jnp.int32)
    vectors = jnp.concatenate([norm_gain, score_gains[0], skip])
    halves = mixer_tables(rate[0], angle[0], coef[0], skip[0], vectors)

    tie = lax.optimization_barrier
    quarters = spread_quarters(out_proj[0], 0, 0)
    own = permuted_rows(inputs[0], order)
    held = (quarters, halves, own, out_proj[0])
    quarters, halves, own, shard = tie(held)

    def along_seq(quarters):
        return {
            section: lax.all_gather(quarter, "seq", axis=0, tiled=True)
            for section, quarter in quarters.items()
        }

    wholes = along_seq(quarters)
    fetched = [across(own_half(halves), hops) for hops in range(1, section_count)]
    last_quarters = spread_quarters(shard, 3, seq_far)
    before = lax.ppermute(own, "seq", [(i, i + 1) for i in range(seq_count - 1)])

    positions = (seq_index - 1) * row_count + jnp.arange(2 * row_count)
    chosen = lax.dynamic_index_in_dim(order, pipe_index, 0, False)
    doc_ends = jnp.cumsum(lax.dynamic_index_in_dim(lengths, chosen, 0, False))
    counted = jnp.sum((doc_ends[None, :] <= positions[:, None]).astype(jnp.int32), axis=1)
    docs = jnp.where(positions >= 0, counted, -1)
    keep, flags = document_flags(docs)

    def hop(section):
        return sent_by_core(wholes[section], (1, 2))

    def mixing(section):
        hops = 2 * (pipe_index ^ section)
        which = jnp.stack([hops + place[1], hops + 1 - place[1]])
        return jnp.concatenate([place, which]), (keep, flags, docs[:, None], docs[None, :], tables)

    near, far = {}, {}
    held = (fetched, before, last_quarters, wholes[0])
    fetched, before, last_quarters, wholes[0] = tie(held)
    near[0] = hop(0)
    tables = joined_tables(halves, fetched)
    where, mixer = mixing(0)
    middle, attended = section_step(where, (before, own), mixing=mixer)
    held = (near[0], middle, attended, wholes[1], last_quarters)
    near[0], middle, attended, wholes[1], last_quarters = tie(held)
    last_quarters = along_seq(last_quarters)
    far[0] = passed_on(near[0], place)
    near[1] = hop(1)
    for section in range(section_count):
        weights = [wholes[section], near[section], swapped(near[section])]
        if section < seq_far:
            far[section], middle, attended = tie((far[section], middle, attended))
            weights += [far[section], swapped(far[section])]
        else:
            weights += [last_quarters[section]]
        if section + 2 < section_count:
            wholes[section + 2], middle, attended = tie((wholes[section + 2], middle, attended))
            near[section + 2] = hop(section + 2)
        if section + 1 < section_count:
            near[section + 1], middle, attended = tie((near[section + 1], middle, attended))
            if section + 1 < seq_far:
                far[section + 1] = passed_on(near[section + 1], place)
            where, mixer = mixing(section + 1)
            with_halo = section + 2 < section_count
            middle, attended = section_step(where, (middle, attended), weights, mixer, with_halo)
    x = section_step(place, (middle, attended), weights)
    return x[None]


def solution(mesh):
    in_specs = (
        P("pipe", "seq", None),
        P(),
        P(),
        P("pipe", None),
        P("pipe", None, None),
        P("pipe", None, None),
        P("pipe", None, None, None),
        P("pipe", None),
        P("pipe", None, None),
        P("pipe", "seq", None),
    )
    out_specs = P("pipe", "seq", None)
    return jax.shard_map(local, mesh=mesh, in_specs=in_specs, out_specs=out_specs, check_vma=False)
```

```python
import functools
import itertools
import math

import jax
import jax.numpy as jnp
import numpy as np
from jax import lax
from jax.experimental import pallas as pl
from jax.experimental.pallas import tpu as pltpu
from jax.sharding import PartitionSpec as P

HEAD_DIM = 128
norm_eps = 1e-06
masked_score = -1e30
lanes = 128
mode_group = 8
chunk_rows = 16
seq_far = 2
head_batch = 8
vector_rows = 4
row_tile = 16


def mixer_tables(rate_now, angle_now, coef_now, skip_now, vectors):
    magnitude = jnp.exp(-rate_now)
    turn_re = magnitude * jnp.cos(angle_now)
    turn_im = magnitude * jnp.sin(angle_now)
    pole_sum = 2.0 * turn_re
    pole_product = -(magnitude * magnitude)
    direct = 2.0 * coef_now[0]
    delayed = -2.0 * (coef_now[0] * turn_re + coef_now[1] * turn_im)
    through = jnp.broadcast_to(skip_now, vectors.shape)
    halves = jnp.stack([
        jnp.concatenate([pole_sum, pole_product, through]),
        jnp.concatenate([direct, delayed, vectors]),
    ])
    return halves.reshape(halves.shape[:2] + (-1, lanes))


def inverse_rms(values):
    return lax.rsqrt(jnp.mean(values * values, axis=1, keepdims=True) + norm_eps)


def fetch(sources, targets, arrived):
    copies = [
        pltpu.make_async_copy(source, target, arrived.at[index])
        for index, (source, target) in enumerate(zip(sources, targets))
    ]
    for copy in copies:
        copy.start()
    return copies


def times(rows, weights):
    return jnp.dot(rows, weights, preferred_element_type=jnp.float32)


def add_projection(place_ref, out_ref, middle_ref, attended_ref, wholes, halves, copies):
    pipe, core = place_ref[0], place_ref[1]
    quarter = wholes.shape[2]

    def put(index, total):
        where = pl.ds(pl.multiple_of(index * quarter, lanes), quarter)
        out_ref[:, where] = (middle_ref[:, where].astype(jnp.float32) + total).astype(jnp.bfloat16)

    for index, hops in zip(range(wholes.shape[0]), (0, 1 + core, 2 - core, 3)):
        copies[index].wait()
        put(pipe ^ hops, times(attended_ref[...], wholes[index]))
    if halves is None:
        return
    half = halves.shape[1]
    total = 0.0
    for index, first in enumerate((core * half, (1 - core) * half)):
        copies[3 + index].wait()
        rows = attended_ref[:, pl.ds(pl.multiple_of(first, lanes), half)]
        total = total + times(rows, halves[index])
    put(pipe ^ 3, total)


def mix_attend(
    keep_ref, broken_ref, doc_col_ref, doc_row_ref, x_ref, pole_ref, zero_ref, middle_ref,
    attended_refs, signal, mixed, queries, keys, with_halo, after_middle, after_half,
):
    rows, width = x_ref.shape
    own = rows // 2
    folds = width // lanes
    modes = (pole_ref.shape[0] - vector_rows) // 2
    heads = width // HEAD_DIM
    tiles = rows // row_tile
    first_chunk = broken_ref[rows // chunk_rows]
    first_tile = first_chunk // (2 * row_tile // chunk_rows) * 2

    def gain(row, fold):
        return zero_ref[2 * modes + row, fold : fold + 1, :]

    def in_pairs(body, first, last):
        def pair(index, carry):
            return body(2 * index + 1, body(2 * index, carry))

        lax.fori_loop(first // 2, last // 2, pair, 0)

    def spread(tile, carry):
        first = pl.multiple_of(tile * row_tile, row_tile)
        plain = x_ref[pl.ds(first, row_tile), :].astype(jnp.float32)
        scaled = plain * inverse_rms(plain)
        for fold in range(folds):
            where = pl.ds(first * folds + fold, row_tile, stride=folds)
            signal[where, :] = scaled[:, fold * lanes : (fold + 1) * lanes] * gain(0, fold)
        return carry

    in_pairs(spread, first_tile, tiles)

    def run_modes(group, opening):
        first_mode = group * mode_group
        coefs = [
            [
                ref[kind * modes + first_mode + index]
                for ref in (pole_ref, zero_ref)
                for kind in range(2)
            ]
            for index in range(mode_group)
        ]
        through = pole_ref[2 * modes] if opening else None

        def advance(chunk, state):
            def steps(state, masked):
                state = list(state)
                for step in range(chunk_rows):
                    row = chunk * chunk_rows + step
                    where = pl.ds(pl.multiple_of(row * folds, folds), folds)
                    entering = signal[where, :]
                    total = through * entering if opening else mixed[where, :]
                    for index in range(mode_group):
                        a1, a2, b0, b1 = coefs[index]
                        newer, older = state[2 * index], state[2 * index + 1]
                        if masked:
                            keep = keep_ref[row]
                            newer, older = newer * keep, older * keep
                        now = (entering + a2 * older) + a1 * newer
                        total = total + (b0 * now + b1 * newer)
                        state[2 * index], state[2 * index + 1] = now, newer
                    mixed[where, :] = total
                return tuple(state)

            return lax.cond(
                broken_ref[chunk] > 0,
                lambda held: steps(held, True),
                lambda held: steps(held, False),
                state,
            )

        zeros = jnp.zeros((folds, lanes), jnp.float32)
        lax.fori_loop(first_chunk, rows // chunk_rows, advance, (zeros,) * (2 * mode_group))

    run_modes(0, True)

    def later_modes(group, carry):
        run_modes(group, False)
        return carry

    lax.fori_loop(1, modes // mode_group, later_modes, 0)

    def gather_back(tile, carry):
        first = pl.multiple_of(tile * row_tile, row_tile)
        where_rows = pl.ds(first, row_tile)
        parts = [
            mixed[pl.ds(first * folds + fold, row_tile, stride=folds), :] for fold in range(folds)
        ]
        plain = x_ref[where_rows, :].astype(jnp.float32)
        middle = (plain + jnp.concatenate(parts, axis=1)).astype(jnp.bfloat16)
        middle_ref[where_rows, :] = middle
        wide = middle.astype(jnp.float32)
        normed = wide * inverse_rms(wide)
        for fold in range(folds):
            part = slice(fold * lanes, (fold + 1) * lanes)
            queries[where_rows, part] = (normed[:, part] * gain(1, fold)).astype(jnp.bfloat16)
            keys[where_rows, part] = (normed[:, part] * gain(2, fold)).astype(jnp.bfloat16)
        return carry

    def clear(tile, carry):
        first = pl.multiple_of(tile * row_tile, row_tile)
        for ref in (middle_ref, queries, keys):
            ref[pl.ds(first, row_tile), :] = jnp.zeros((row_tile, width), jnp.bfloat16)
        return carry

    in_pairs(clear, 0, first_tile)
    in_pairs(gather_back, first_tile, tiles)
    after_middle()

    query_pos = lax.broadcasted_iota(jnp.int32, (own, rows), 0) + own
    key_pos = lax.broadcasted_iota(jnp.int32, (own, rows), 1)
    allowed_own = (key_pos <= query_pos) & (doc_col_ref[own:, :] == doc_row_ref[...])
    allowed_halo = (key_pos[:, :own] <= query_pos[:, :own] - own) & (
        doc_col_ref[:own, :] == doc_row_ref[:, :own]
    )
    rate = HEAD_DIM ** (-0.5) * math.log2(math.e)
    blocks = [(own, rows, allowed_own)]
    if with_halo:
        blocks.insert(0, (0, own, allowed_halo))
    skipped = rows - own * len(blocks)
    for batch in range(0, heads, head_batch):
        jobs = [
            (head, first, count, allowed)
            for head in range(batch, batch + head_batch)
            for first, count, allowed in blocks
        ]
        raws = []
        for head, first, count, allowed in jobs:
            where = slice(head * HEAD_DIM, (head + 1) * HEAD_DIM)
            scores = lax.dot_general(
                queries[first : first + own, where], keys[:count, where], (((1,), (1,)), ((), ())),
                preferred_element_type=jnp.float32,
            )
            raws.append(jnp.where(allowed, scores, masked_score))
        tops = [jnp.max(raw, axis=1, keepdims=True) for raw in raws]
        raws = [jnp.exp2((raw - top) * rate) for raw, top in zip(raws, tops)]
        sums = [jnp.sum(raw, axis=1, keepdims=True) for raw in raws]
        raws = [(raw * (1.0 / total)).astype(jnp.bfloat16) for raw, total in zip(raws, sums)]
        for (head, first, count, _), weights in zip(jobs, raws):
            where = slice(head * HEAD_DIM, (head + 1) * HEAD_DIM)
            part, inner = divmod(head, heads // 2)
            placed = slice(inner * HEAD_DIM, (inner + 1) * HEAD_DIM)
            attended_refs[part][first - skipped : first - skipped + own, placed] = times(
                weights, middle_ref[:count, where]
            ).astype(jnp.bfloat16)
        if (batch + head_batch) % (heads // 2) == 0:
            after_half(batch // (heads // 2))


def section_kernel(wholes_count, halves_count, mixes, with_halo, *refs):
    refs = list(refs)

    def take(count):
        taken, refs[:count] = refs[:count], []
        return taken

    place_ref, = take(1)
    if mixes:
        keep_ref, broken_ref, doc_col_ref, doc_row_ref, tables_ref = take(5)
    sources, weights = take(2), take(wholes_count + halves_count)
    if mixes:
        middle_out, attended_out = take(2)
    else:
        out_ref, = take(1)
    arrived, = take(1)
    if mixes:
        x_ref, pole_ref, zero_ref, middle_ref, low_ref, high_ref, signal, mixed, queries, keys = take(10)
        copies = fetch(
            [tables_ref.at[place_ref[2]], tables_ref.at[place_ref[3]]], [pole_ref, zero_ref],
            arrived.at[pl.ds(10, 2)],
        )
    if weights:
        middle_in, attended_in, wholes = take(3)
        halves = take(1)[0] if halves_count else None
        skipped = sources[0].shape[0] - middle_in.shape[0]
        rows = pl.ds(skipped, middle_in.shape[0])
        inputs = fetch([source.at[rows] for source in sources], [middle_in, attended_in], arrived)
        targets = [wholes.at[index] for index in range(wholes_count)]
        targets += [halves.at[index] for index in range(halves_count)]
        pieces = fetch(weights, targets, arrived.at[pl.ds(2, 5)])
        for copy in inputs:
            copy.wait()
        target = x_ref if mixes else out_ref
        add_projection(place_ref, target, middle_in, attended_in, wholes, halves, pieces)
    else:
        own = x_ref.shape[0] // 2
        inputs = fetch(sources, [x_ref.at[pl.ds(0, own)], x_ref.at[pl.ds(own, own)]], arrived)
        for copy in inputs:
            copy.wait()
    if not mixes:
        return
    for copy in copies:
        copy.wait()
    skipped = middle_ref.shape[0] - middle_out.shape[0]
    half = low_ref.shape[1]
    results = [
        pltpu.make_async_copy(
            middle_ref.at[pl.ds(skipped, middle_out.shape[0])], middle_out, arrived.at[7]
        )
    ] + [
        pltpu.make_async_copy(
            ref, attended_out.at[:, pl.ds(index * half, half)], arrived.at[8 + index]
        )
        for index, ref in enumerate((low_ref, high_ref))
    ]
    mix_attend(
        keep_ref, broken_ref, doc_col_ref, doc_row_ref, x_ref, pole_ref, zero_ref, middle_ref,
        (low_ref, high_ref), signal, mixed, queries, keys, with_halo,
        results[0].start, lambda part: results[1 + part].start(),
    )
    for copy in results:
        copy.wait()


def section_step(place, sources, weights=(), mixing=(), with_halo=True):
    width = sources[0].shape[1]
    smem, vmem, anywhere = (
        pl.BlockSpec(memory_space=space) for space in (pltpu.SMEM, pltpu.VMEM, pltpu.HBM)
    )
    rows = sources[0].shape[0] if weights else 2 * sources[0].shape[0]
    folds = width // lanes
    wholes_count = sum(weight.shape[0] == width for weight in weights)
    halves_count = len(weights) - wholes_count
    scratch = [pltpu.SemaphoreType.DMA((12,))]
    if mixing:
        kept = rows if with_halo else rows // 2
        wide = pltpu.VMEM((rows * folds, lanes), jnp.float32)
        narrow = pltpu.VMEM((rows, width), jnp.bfloat16)
        half = pltpu.VMEM((kept, width // 2), jnp.bfloat16)
        table = pltpu.VMEM(mixing[-1].shape[1:], jnp.float32)
        scratch += [narrow, table, table, narrow, half, half, wide, wide, narrow, narrow]
        out_shape = [jax.ShapeDtypeStruct((kept, width), jnp.bfloat16)] * 2
        out_specs = [anywhere, anywhere]
    else:
        kept = rows
        out_shape = jax.ShapeDtypeStruct((rows, width), jnp.bfloat16)
        out_specs = vmem
    if weights:
        held = pltpu.VMEM((rows, width), jnp.bfloat16)
        scratch += [
            held, held,
            pltpu.VMEM((wholes_count,) + weights[0].shape, jnp.bfloat16),
        ]
        if halves_count:
            scratch.append(pltpu.VMEM((halves_count,) + weights[-1].shape, jnp.bfloat16))
    return pl.pallas_call(
        functools.partial(section_kernel, wholes_count, halves_count, bool(mixing), with_halo),
        out_shape=out_shape,
        in_specs=[smem]
        + ([smem, smem, vmem, vmem, anywhere] if mixing else [])
        + [anywhere] * (len(sources) + len(weights)),
        out_specs=out_specs,
        scratch_shapes=scratch,
        compiler_params=pltpu.CompilerParams(vmem_limit_bytes=60 << 20),
        cost_estimate=pl.CostEstimate(
            flops=2 * rows * width * width, bytes_accessed=2 * width * width, transcendentals=0
        ),
        name="section_step",
    )(place, *mixing, *sources, *weights)


def half_copy_kernel(place_ref, value_ref, out_ref, held, arrived, left):
    half = out_ref.shape[0]
    part = half // 4
    parts = [pl.ds(index * part, part) for index in range(4)]
    starts = [place_ref[1] * half + index * part for index in range(4)]
    sources = [value_ref.at[pl.ds(first, part)] for first in starts]
    coming = fetch(sources, [held.at[where] for where in parts], arrived)
    going = []
    for index, where in enumerate(parts):
        coming[index].wait()
        going.append(pltpu.make_async_copy(held.at[where], out_ref.at[where], left.at[index]))
        going[-1].start()
    for copy in going:
        copy.wait()


def core_half(value, place):
    hbm = pl.BlockSpec(memory_space=pltpu.HBM)
    shape = (value.shape[0] // 2,) + value.shape[1:]
    return pl.pallas_call(
        half_copy_kernel,
        out_shape=jax.ShapeDtypeStruct(shape, value.dtype),
        in_specs=[pl.BlockSpec(memory_space=pltpu.SMEM), hbm],
        out_specs=hbm,
        scratch_shapes=[pltpu.VMEM(shape, value.dtype)] + [pltpu.SemaphoreType.DMA((4,))] * 2,
        compiler_params=pltpu.CompilerParams(vmem_limit_bytes=60 << 20),
        name="core_half",
    )(place, value)


def document_flags(docs):
    goes_on = jnp.concatenate([jnp.zeros((1,), bool), docs[1:] == docs[:-1]])
    broken = jnp.any(jnp.logical_not(goes_on).reshape(-1, chunk_rows), axis=1)
    needed = docs == docs[docs.shape[0] // 2]
    first_chunk = jnp.argmax(needed) // chunk_rows
    flags = jnp.concatenate([broken.astype(jnp.int32), first_chunk.astype(jnp.int32)[None]])
    return goes_on.astype(jnp.float32), flags


def across(value, hops):
    count = lax.axis_size("pipe")
    return lax.ppermute(value, "pipe", [(i, i ^ hops) for i in range(count)])


def swapped(value):
    count = lax.axis_size("seq")
    return lax.ppermute(value, "seq", [(i, i ^ 1) for i in range(count)])


def spread_quarters(shard, offset, first):
    section_count = lax.axis_size("pipe")
    pipe_index = lax.axis_index("pipe")
    quarter = shard.shape[1] // section_count

    def columns(hops):
        return lax.dynamic_slice_in_dim(shard, (pipe_index ^ hops ^ offset) * quarter, quarter, 1)

    held = [columns(0)]
    for hops in range(1, section_count):
        pairs = [(i, i ^ hops) for i in range(first, section_count)]
        held.append(lax.ppermute(columns(hops), "pipe", pairs))
    held = jnp.stack(held)
    return {
        section: lax.dynamic_index_in_dim(held, pipe_index ^ section, 0, False)
        for section in range(first, section_count)
    }


def own_half(halves):
    return lax.dynamic_index_in_dim(halves, lax.axis_index("seq") % 2, 0, False)


def joined_tables(halves, fetched):
    fetched = jnp.stack(fetched)
    other = swapped(fetched)
    own = jnp.where(lax.axis_index("seq") % 2 == 0, halves, halves[::-1])
    return jnp.concatenate([own, jnp.stack([fetched, other], axis=1).reshape((-1,) + own.shape[1:])])


def sent_by_core(value, hops_by_core):
    pipe_count, seq_count = lax.axis_size("pipe"), lax.axis_size("seq")
    pairs = [
        (pipe * seq_count + seq, (pipe ^ hops_by_core[seq % 2]) * seq_count + seq)
        for pipe in range(pipe_count)
        for seq in range(seq_count)
    ]
    return lax.ppermute(value, ("pipe", "seq"), pairs)


def passed_on(fetched, place):
    return sent_by_core(core_half(fetched, place), (2, 1))


def permuted_rows(value, order):
    count = lax.axis_size("pipe")
    choices = list(itertools.permutations(range(count)))
    match = jnp.all(jnp.asarray(np.array(choices, np.int32)) == order[None, :], axis=1)
    which = jnp.argmax(match).astype(jnp.int32)

    def mover(choice):
        pairs = [(source, target) for target, source in enumerate(choice)]
        return lambda held: lax.ppermute(held, "pipe", pairs)

    return lax.switch(which, [mover(choice) for choice in choices], value)


def local(inputs, lengths, order, norm_gain, rate, angle, coef, skip, score_gains, out_proj):
    section_count = lax.axis_size("pipe")
    seq_count = lax.axis_size("seq")
    pipe_index = lax.axis_index("pipe")
    seq_index = lax.axis_index("seq")
    row_count = inputs.shape[1]

    place = jnp.stack([pipe_index, seq_index % 2]).astype(jnp.int32)
    vectors = jnp.concatenate([norm_gain, score_gains[0], skip])
    halves = mixer_tables(rate[0], angle[0], coef[0], skip[0], vectors)

    tie = lax.optimization_barrier
    quarters = spread_quarters(out_proj[0], 0, 0)
    held = (quarters, halves, inputs[0], out_proj[0])
    quarters, halves, entering, shard = tie(held)

    def along_seq(quarters):
        return {
            section: lax.all_gather(quarter, "seq", axis=0, tiled=True)
            for section, quarter in quarters.items()
        }

    wholes = along_seq(quarters)
    own, halves, shard = tie((permuted_rows(entering, order), halves, shard))
    fetched = [across(own_half(halves), hops) for hops in range(1, section_count)]
    last_quarters = spread_quarters(shard, 3, seq_far)
    before = lax.ppermute(own, "seq", [(i, i + 1) for i in range(seq_count - 1)])

    positions = (seq_index - 1) * row_count + jnp.arange(2 * row_count)
    chosen = lax.dynamic_index_in_dim(order, pipe_index, 0, False)
    doc_ends = jnp.cumsum(lax.dynamic_index_in_dim(lengths, chosen, 0, False))
    counted = jnp.sum((doc_ends[None, :] <= positions[:, None]).astype(jnp.int32), axis=1)
    docs = jnp.where(positions >= 0, counted, -1)
    keep, flags = document_flags(docs)

    def hop(section):
        return sent_by_core(wholes[section], (1, 2))

    def mixing(section):
        hops = 2 * (pipe_index ^ section)
        which = jnp.stack([hops + place[1], hops + 1 - place[1]])
        return jnp.concatenate([place, which]), (keep, flags, docs[:, None], docs[None, :], tables)

    near, far = {}, {}
    fetched, wholes[0] = tie((fetched, wholes[0]))
    near[0] = hop(0)
    held = (near[0], wholes[1], own, before, fetched, last_quarters)
    near[0], wholes[1], own, before, fetched, last_quarters = tie(held)
    half = core_half(near[0], place)
    half, own, before, fetched, halves = tie((half, own, before, fetched, halves))
    far[0] = sent_by_core(half, (2, 1))
    near[1] = hop(1)
    last_quarters = along_seq(last_quarters)
    tables = joined_tables(halves, fetched)
    where, mixer = mixing(0)
    middle, attended = section_step(where, (before, own), mixing=mixer)
    for section in range(section_count):
        weights = [wholes[section], near[section], swapped(near[section])]
        if section < seq_far:
            far[section], middle, attended = tie((far[section], middle, attended))
            weights += [far[section], swapped(far[section])]
        else:
            weights += [last_quarters[section]]
        if section + 2 < section_count:
            wholes[section + 2], middle, attended = tie((wholes[section + 2], middle, attended))
            near[section + 2] = hop(section + 2)
        if section + 1 < section_count:
            near[section + 1], middle, attended = tie((near[section + 1], middle, attended))
            if section + 1 < seq_far:
                far[section + 1] = passed_on(near[section + 1], place)
            where, mixer = mixing(section + 1)
            with_halo = section + 2 < section_count
            middle, attended = section_step(where, (middle, attended), weights, mixer, with_halo)
    x = section_step(place, (middle, attended), weights)
    return x[None]


def solution(mesh):
    in_specs = (
        P("pipe", "seq", None),
        P(),
        P(),
        P("pipe", None),
        P("pipe", None, None),
        P("pipe", None, None),
        P("pipe", None, None, None),
        P("pipe", None),
        P("pipe", None, None),
        P("pipe", "seq", None),
    )
    out_specs = P("pipe", "seq", None)
    return jax.shard_map(local, mesh=mesh, in_specs=in_specs, out_specs=out_specs, check_vma=False)
```

```python
import functools
import itertools
import math

import jax
import jax.numpy as jnp
import numpy as np
from jax import lax
from jax.experimental import pallas as pl
from jax.experimental.pallas import tpu as pltpu
from jax.sharding import PartitionSpec as P

HEAD_DIM = 128
norm_eps = 1e-06
masked_score = -1e30
lanes = 128
mode_group = 8
seq_far = 2
head_batch = 8
vector_rows = 4
row_tile = 16
chunk_rows = row_tile


def mixer_tables(rate_now, angle_now, coef_now, skip_now, vectors):
    magnitude = jnp.exp(-rate_now)
    turn_re = magnitude * jnp.cos(angle_now)
    turn_im = magnitude * jnp.sin(angle_now)
    pole_sum = 2.0 * turn_re
    pole_product = -(magnitude * magnitude)
    direct = 2.0 * coef_now[0]
    delayed = -2.0 * (coef_now[0] * turn_re + coef_now[1] * turn_im)
    through = jnp.broadcast_to(skip_now, vectors.shape)
    halves = jnp.stack([
        jnp.concatenate([pole_sum, pole_product, through]),
        jnp.concatenate([direct, delayed, vectors]),
    ])
    return halves.reshape(halves.shape[:2] + (-1, lanes))


def inverse_rms(values):
    return lax.rsqrt(jnp.mean(values * values, axis=1, keepdims=True) + norm_eps)


def fetch(sources, targets, arrived):
    copies = [
        pltpu.make_async_copy(source, target, arrived.at[index])
        for index, (source, target) in enumerate(zip(sources, targets))
    ]
    for copy in copies:
        copy.start()
    return copies


def times(rows, weights):
    return jnp.dot(rows, weights, preferred_element_type=jnp.float32)


def add_projection(place_ref, out_ref, middle_ref, attended_ref, wholes, halves, copies):
    pipe, core = place_ref[0], place_ref[1]
    quarter = wholes.shape[2]

    def put(index, total):
        where = pl.ds(pl.multiple_of(index * quarter, lanes), quarter)
        out_ref[:, where] = (middle_ref[:, where].astype(jnp.float32) + total).astype(jnp.bfloat16)

    for index, hops in zip(range(wholes.shape[0]), (0, 1 + core, 2 - core, 3)):
        copies[index].wait()
        put(pipe ^ hops, times(attended_ref[...], wholes[index]))
    if halves is None:
        return
    half = halves.shape[1]
    total = 0.0
    for index, first in enumerate((core * half, (1 - core) * half)):
        copies[3 + index].wait()
        rows = attended_ref[:, pl.ds(pl.multiple_of(first, lanes), half)]
        total = total + times(rows, halves[index])
    put(pipe ^ 3, total)


def mix_attend(
    keep_ref, broken_ref, doc_col_ref, doc_row_ref, x_ref, pole_ref, zero_ref, middle_ref,
    attended_refs, signal, mixed, queries, keys, with_halo, after_middle, after_half,
):
    rows, width = x_ref.shape
    own = rows // 2
    folds = width // lanes
    modes = (pole_ref.shape[0] - vector_rows) // 2
    heads = width // HEAD_DIM
    tiles = rows // row_tile
    first_chunk = broken_ref[rows // chunk_rows]
    first_tile = first_chunk // 2 * 2

    @pl.when(first_chunk > first_tile)
    def _():
        blank = pl.ds(pl.multiple_of(first_tile * row_tile * folds, row_tile * folds), row_tile * folds)
        mixed[blank, :] = jnp.zeros((row_tile * folds, lanes), jnp.float32)

    def gain(row, fold):
        return zero_ref[2 * modes + row, fold : fold + 1, :]

    def in_pairs(body, first, last):
        def pair(index, carry):
            return body(2 * index + 1, body(2 * index, carry))

        lax.fori_loop(first // 2, last // 2, pair, 0)

    def spread(tile, carry):
        first = pl.multiple_of(tile * row_tile, row_tile)
        plain = x_ref[pl.ds(first, row_tile), :].astype(jnp.float32)
        scaled = plain * inverse_rms(plain)
        for fold in range(folds):
            where = pl.ds(first * folds + fold, row_tile, stride=folds)
            signal[where, :] = scaled[:, fold * lanes : (fold + 1) * lanes] * gain(0, fold)
        return carry

    in_pairs(spread, first_tile, tiles)

    def run_modes(group, opening):
        first_mode = group * mode_group
        coefs = [
            [
                ref[kind * modes + first_mode + index]
                for ref in (pole_ref, zero_ref)
                for kind in range(2)
            ]
            for index in range(mode_group)
        ]
        through = pole_ref[2 * modes] if opening else None

        def advance(chunk, state):
            def steps(state, masked):
                state = list(state)
                for step in range(chunk_rows):
                    row = chunk * chunk_rows + step
                    where = pl.ds(pl.multiple_of(row * folds, folds), folds)
                    entering = signal[where, :]
                    total = through * entering if opening else mixed[where, :]
                    for index in range(mode_group):
                        a1, a2, b0, b1 = coefs[index]
                        newer, older = state[2 * index], state[2 * index + 1]
                        if masked:
                            keep = keep_ref[row]
                            newer, older = newer * keep, older * keep
                        now = (entering + a2 * older) + a1 * newer
                        total = total + (b0 * now + b1 * newer)
                        state[2 * index], state[2 * index + 1] = now, newer
                    mixed[where, :] = total
                return tuple(state)

            return lax.cond(
                broken_ref[chunk] > 0,
                lambda held: steps(held, True),
                lambda held: steps(held, False),
                state,
            )

        zeros = jnp.zeros((folds, lanes), jnp.float32)
        lax.fori_loop(first_chunk, rows // chunk_rows, advance, (zeros,) * (2 * mode_group))

    run_modes(0, True)

    def later_modes(group, carry):
        run_modes(group, False)
        return carry

    lax.fori_loop(1, modes // mode_group, later_modes, 0)

    def gather_back(tile, carry):
        first = pl.multiple_of(tile * row_tile, row_tile)
        where_rows = pl.ds(first, row_tile)
        parts = [
            mixed[pl.ds(first * folds + fold, row_tile, stride=folds), :] for fold in range(folds)
        ]
        plain = x_ref[where_rows, :].astype(jnp.float32)
        middle = (plain + jnp.concatenate(parts, axis=1)).astype(jnp.bfloat16)
        middle_ref[where_rows, :] = middle
        wide = middle.astype(jnp.float32)
        normed = wide * inverse_rms(wide)
        for fold in range(folds):
            part = slice(fold * lanes, (fold + 1) * lanes)
            queries[where_rows, part] = (normed[:, part] * gain(1, fold)).astype(jnp.bfloat16)
            keys[where_rows, part] = (normed[:, part] * gain(2, fold)).astype(jnp.bfloat16)
        return carry

    def clear(tile, carry):
        first = pl.multiple_of(tile * row_tile, row_tile)
        for ref in (middle_ref, queries, keys):
            ref[pl.ds(first, row_tile), :] = jnp.zeros((row_tile, width), jnp.bfloat16)
        return carry

    in_pairs(clear, 0, first_tile)
    in_pairs(gather_back, first_tile, tiles)
    after_middle()

    query_pos = lax.broadcasted_iota(jnp.int32, (own, rows), 0) + own
    key_pos = lax.broadcasted_iota(jnp.int32, (own, rows), 1)
    allowed_own = (key_pos <= query_pos) & (doc_col_ref[own:, :] == doc_row_ref[...])
    allowed_halo = (key_pos[:, :own] <= query_pos[:, :own] - own) & (
        doc_col_ref[:own, :] == doc_row_ref[:, :own]
    )
    rate = HEAD_DIM ** (-0.5) * math.log2(math.e)
    blocks = [(own, rows, allowed_own)]
    if with_halo:
        blocks.insert(0, (0, own, allowed_halo))
    skipped = rows - own * len(blocks)
    for batch in range(0, heads, head_batch):
        jobs = [
            (head, first, count, allowed)
            for head in range(batch, batch + head_batch)
            for first, count, allowed in blocks
        ]
        raws = []
        for head, first, count, allowed in jobs:
            where = slice(head * HEAD_DIM, (head + 1) * HEAD_DIM)
            scores = lax.dot_general(
                queries[first : first + own, where], keys[:count, where], (((1,), (1,)), ((), ())),
                preferred_element_type=jnp.float32,
            )
            raws.append(jnp.where(allowed, scores, masked_score))
        tops = [jnp.max(raw, axis=1, keepdims=True) for raw in raws]
        raws = [jnp.exp2((raw - top) * rate) for raw, top in zip(raws, tops)]
        sums = [jnp.sum(raw, axis=1, keepdims=True) for raw in raws]
        raws = [(raw * (1.0 / total)).astype(jnp.bfloat16) for raw, total in zip(raws, sums)]
        for (head, first, count, _), weights in zip(jobs, raws):
            where = slice(head * HEAD_DIM, (head + 1) * HEAD_DIM)
            part, inner = divmod(head, heads // 2)
            placed = slice(inner * HEAD_DIM, (inner + 1) * HEAD_DIM)
            attended_refs[part][first - skipped : first - skipped + own, placed] = times(
                weights, middle_ref[:count, where]
            ).astype(jnp.bfloat16)
        if (batch + head_batch) % (heads // 2) == 0:
            after_half(batch // (heads // 2))


def section_kernel(wholes_count, halves_count, mixes, with_halo, *refs):
    refs = list(refs)

    def take(count):
        taken, refs[:count] = refs[:count], []
        return taken

    place_ref, = take(1)
    if mixes:
        keep_ref, broken_ref, doc_col_ref, doc_row_ref, tables_ref = take(5)
    sources, weights = take(2), take(wholes_count + halves_count)
    if mixes:
        middle_out, attended_out = take(2)
    else:
        out_ref, = take(1)
    arrived, = take(1)
    if mixes:
        x_ref, pole_ref, zero_ref, middle_ref, low_ref, high_ref, signal, mixed, queries, keys = take(10)
        copies = fetch(
            [tables_ref.at[place_ref[2]], tables_ref.at[place_ref[3]]], [pole_ref, zero_ref],
            arrived.at[pl.ds(10, 2)],
        )
    if weights:
        middle_in, attended_in, wholes = take(3)
        halves = take(1)[0] if halves_count else None
        skipped = sources[0].shape[0] - middle_in.shape[0]
        rows = pl.ds(skipped, middle_in.shape[0])
        inputs = fetch([source.at[rows] for source in sources], [middle_in, attended_in], arrived)
        targets = [wholes.at[index] for index in range(wholes_count)]
        targets += [halves.at[index] for index in range(halves_count)]
        pieces = fetch(weights, targets, arrived.at[pl.ds(2, 5)])
        for copy in inputs:
            copy.wait()
        target = x_ref if mixes else out_ref
        add_projection(place_ref, target, middle_in, attended_in, wholes, halves, pieces)
    else:
        own = x_ref.shape[0] // 2
        inputs = fetch(sources, [x_ref.at[pl.ds(0, own)], x_ref.at[pl.ds(own, own)]], arrived)
        for copy in inputs:
            copy.wait()
    if not mixes:
        return
    for copy in copies:
        copy.wait()
    skipped = middle_ref.shape[0] - middle_out.shape[0]
    half = low_ref.shape[1]
    results = [
        pltpu.make_async_copy(
            middle_ref.at[pl.ds(skipped, middle_out.shape[0])], middle_out, arrived.at[7]
        )
    ] + [
        pltpu.make_async_copy(
            ref, attended_out.at[:, pl.ds(index * half, half)], arrived.at[8 + index]
        )
        for index, ref in enumerate((low_ref, high_ref))
    ]
    mix_attend(
        keep_ref, broken_ref, doc_col_ref, doc_row_ref, x_ref, pole_ref, zero_ref, middle_ref,
        (low_ref, high_ref), signal, mixed, queries, keys, with_halo,
        results[0].start, lambda part: results[1 + part].start(),
    )
    for copy in results:
        copy.wait()


def section_step(place, sources, weights=(), mixing=(), with_halo=True):
    width = sources[0].shape[1]
    smem, vmem, anywhere = (
        pl.BlockSpec(memory_space=space) for space in (pltpu.SMEM, pltpu.VMEM, pltpu.HBM)
    )
    rows = sources[0].shape[0] if weights else 2 * sources[0].shape[0]
    folds = width // lanes
    wholes_count = sum(weight.shape[0] == width for weight in weights)
    halves_count = len(weights) - wholes_count
    scratch = [pltpu.SemaphoreType.DMA((12,))]
    if mixing:
        kept = rows if with_halo else rows // 2
        wide = pltpu.VMEM((rows * folds, lanes), jnp.float32)
        narrow = pltpu.VMEM((rows, width), jnp.bfloat16)
        half = pltpu.VMEM((kept, width // 2), jnp.bfloat16)
        table = pltpu.VMEM(mixing[-1].shape[1:], jnp.float32)
        scratch += [narrow, table, table, narrow, half, half, wide, wide, narrow, narrow]
        out_shape = [jax.ShapeDtypeStruct((kept, width), jnp.bfloat16)] * 2
        out_specs = [anywhere, anywhere]
    else:
        kept = rows
        out_shape = jax.ShapeDtypeStruct((rows, width), jnp.bfloat16)
        out_specs = vmem
    if weights:
        held = pltpu.VMEM((rows, width), jnp.bfloat16)
        scratch += [
            held, held,
            pltpu.VMEM((wholes_count,) + weights[0].shape, jnp.bfloat16),
        ]
        if halves_count:
            scratch.append(pltpu.VMEM((halves_count,) + weights[-1].shape, jnp.bfloat16))
    return pl.pallas_call(
        functools.partial(section_kernel, wholes_count, halves_count, bool(mixing), with_halo),
        out_shape=out_shape,
        in_specs=[smem]
        + ([smem, smem, vmem, vmem, anywhere] if mixing else [])
        + [anywhere] * (len(sources) + len(weights)),
        out_specs=out_specs,
        scratch_shapes=scratch,
        compiler_params=pltpu.CompilerParams(vmem_limit_bytes=60 << 20),
        cost_estimate=pl.CostEstimate(
            flops=2 * rows * width * width, bytes_accessed=2 * width * width, transcendentals=0
        ),
        name="section_step",
    )(place, *mixing, *sources, *weights)


def half_copy_kernel(place_ref, value_ref, out_ref, held, arrived, left):
    half = out_ref.shape[0]
    part = half // 4
    parts = [pl.ds(index * part, part) for index in range(4)]
    starts = [place_ref[1] * half + index * part for index in range(4)]
    sources = [value_ref.at[pl.ds(first, part)] for first in starts]
    coming = fetch(sources, [held.at[where] for where in parts], arrived)
    going = []
    for index, where in enumerate(parts):
        coming[index].wait()
        going.append(pltpu.make_async_copy(held.at[where], out_ref.at[where], left.at[index]))
        going[-1].start()
    for copy in going:
        copy.wait()


def core_half(value, place):
    hbm = pl.BlockSpec(memory_space=pltpu.HBM)
    shape = (value.shape[0] // 2,) + value.shape[1:]
    return pl.pallas_call(
        half_copy_kernel,
        out_shape=jax.ShapeDtypeStruct(shape, value.dtype),
        in_specs=[pl.BlockSpec(memory_space=pltpu.SMEM), hbm],
        out_specs=hbm,
        scratch_shapes=[pltpu.VMEM(shape, value.dtype)] + [pltpu.SemaphoreType.DMA((4,))] * 2,
        compiler_params=pltpu.CompilerParams(vmem_limit_bytes=60 << 20),
        name="core_half",
    )(place, value)


def document_flags(docs):
    goes_on = jnp.concatenate([jnp.zeros((1,), bool), docs[1:] == docs[:-1]])
    broken = jnp.any(jnp.logical_not(goes_on).reshape(-1, chunk_rows), axis=1)
    needed = docs == docs[docs.shape[0] // 2]
    first_chunk = jnp.argmax(needed) // chunk_rows
    flags = jnp.concatenate([broken.astype(jnp.int32), first_chunk.astype(jnp.int32)[None]])
    return goes_on.astype(jnp.float32), flags


def across(value, hops):
    count = lax.axis_size("pipe")
    return lax.ppermute(value, "pipe", [(i, i ^ hops) for i in range(count)])


def swapped(value):
    count = lax.axis_size("seq")
    return lax.ppermute(value, "seq", [(i, i ^ 1) for i in range(count)])


def spread_quarters(shard, offset, first):
    section_count = lax.axis_size("pipe")
    pipe_index = lax.axis_index("pipe")
    quarter = shard.shape[1] // section_count

    def columns(hops):
        return lax.dynamic_slice_in_dim(shard, (pipe_index ^ hops ^ offset) * quarter, quarter, 1)

    held = [columns(0)]
    for hops in range(1, section_count):
        pairs = [(i, i ^ hops) for i in range(first, section_count)]
        held.append(lax.ppermute(columns(hops), "pipe", pairs))
    held = jnp.stack(held)
    return {
        section: lax.dynamic_index_in_dim(held, pipe_index ^ section, 0, False)
        for section in range(first, section_count)
    }


def own_half(halves):
    return lax.dynamic_index_in_dim(halves, lax.axis_index("seq") % 2, 0, False)


def joined_tables(halves, fetched):
    fetched = jnp.stack(fetched)
    other = swapped(fetched)
    own = jnp.where(lax.axis_index("seq") % 2 == 0, halves, halves[::-1])
    return jnp.concatenate([own, jnp.stack([fetched, other], axis=1).reshape((-1,) + own.shape[1:])])


def sent_by_core(value, hops_by_core):
    pipe_count, seq_count = lax.axis_size("pipe"), lax.axis_size("seq")
    pairs = [
        (pipe * seq_count + seq, (pipe ^ hops_by_core[seq % 2]) * seq_count + seq)
        for pipe in range(pipe_count)
        for seq in range(seq_count)
    ]
    return lax.ppermute(value, ("pipe", "seq"), pairs)


def passed_on(fetched, place):
    return sent_by_core(core_half(fetched, place), (2, 1))


def permuted_rows(value, order):
    count = lax.axis_size("pipe")
    choices = list(itertools.permutations(range(count)))
    match = jnp.all(jnp.asarray(np.array(choices, np.int32)) == order[None, :], axis=1)
    which = jnp.argmax(match).astype(jnp.int32)

    def mover(choice):
        pairs = [(source, target) for target, source in enumerate(choice)]
        return lambda held: lax.ppermute(held, "pipe", pairs)

    return lax.switch(which, [mover(choice) for choice in choices], value)


def local(inputs, lengths, order, norm_gain, rate, angle, coef, skip, score_gains, out_proj):
    section_count = lax.axis_size("pipe")
    seq_count = lax.axis_size("seq")
    pipe_index = lax.axis_index("pipe")
    seq_index = lax.axis_index("seq")
    row_count = inputs.shape[1]

    place = jnp.stack([pipe_index, seq_index % 2]).astype(jnp.int32)
    vectors = jnp.concatenate([norm_gain, score_gains[0], skip])
    halves = mixer_tables(rate[0], angle[0], coef[0], skip[0], vectors)

    tie = lax.optimization_barrier
    quarters = spread_quarters(out_proj[0], 0, 0)
    held = (quarters, halves, inputs[0], out_proj[0])
    quarters, halves, entering, shard = tie(held)

    def along_seq(quarters):
        return {
            section: lax.all_gather(quarter, "seq", axis=0, tiled=True)
            for section, quarter in quarters.items()
        }

    wholes = along_seq(quarters)
    own, halves, shard = tie((permuted_rows(entering, order), halves, shard))
    fetched = [across(own_half(halves), hops) for hops in range(1, section_count)]
    last_quarters = spread_quarters(shard, 3, seq_far)
    before = lax.ppermute(own, "seq", [(i, i + 1) for i in range(seq_count - 1)])

    positions = (seq_index - 1) * row_count + jnp.arange(2 * row_count)
    chosen = lax.dynamic_index_in_dim(order, pipe_index, 0, False)
    doc_ends = jnp.cumsum(lax.dynamic_index_in_dim(lengths, chosen, 0, False))
    counted = jnp.sum((doc_ends[None, :] <= positions[:, None]).astype(jnp.int32), axis=1)
    docs = jnp.where(positions >= 0, counted, -1)
    keep, flags = document_flags(docs)

    def hop(section):
        return sent_by_core(wholes[section], (1, 2))

    def mixing(section):
        hops = 2 * (pipe_index ^ section)
        which = jnp.stack([hops + place[1], hops + 1 - place[1]])
        return jnp.concatenate([place, which]), (keep, flags, docs[:, None], docs[None, :], tables)

    near, far = {}, {}
    fetched, wholes[0] = tie((fetched, wholes[0]))
    near[0] = hop(0)
    held = (near[0], wholes[1], own, before, fetched, last_quarters)
    near[0], wholes[1], own, before, fetched, last_quarters = tie(held)
    half = core_half(near[0], place)
    half, own, before, fetched, halves = tie((half, own, before, fetched, halves))
    far[0] = sent_by_core(half, (2, 1))
    near[1] = hop(1)
    last_quarters = along_seq(last_quarters)
    tables = joined_tables(halves, fetched)
    where, mixer = mixing(0)
    middle, attended = section_step(where, (before, own), mixing=mixer)
    for section in range(section_count):
        weights = [wholes[section], near[section], swapped(near[section])]
        if section < seq_far:
            far[section], middle, attended = tie((far[section], middle, attended))
            weights += [far[section], swapped(far[section])]
        else:
            weights += [last_quarters[section]]
        if section + 2 < section_count:
            wholes[section + 2], middle, attended = tie((wholes[section + 2], middle, attended))
            near[section + 2] = hop(section + 2)
        if section + 1 < section_count:
            near[section + 1], middle, attended = tie((near[section + 1], middle, attended))
            if section + 1 < seq_far:
                far[section + 1] = passed_on(near[section + 1], place)
            where, mixer = mixing(section + 1)
            with_halo = section + 2 < section_count
            middle, attended = section_step(where, (middle, attended), weights, mixer, with_halo)
    x = section_step(place, (middle, attended), weights)
    return x[None]


def solution(mesh):
    in_specs = (
        P("pipe", "seq", None),
        P(),
        P(),
        P("pipe", None),
        P("pipe", None, None),
        P("pipe", None, None),
        P("pipe", None, None, None),
        P("pipe", None),
        P("pipe", None, None),
        P("pipe", "seq", None),
    )
    out_specs = P("pipe", "seq", None)
    return jax.shard_map(local, mesh=mesh, in_specs=in_specs, out_specs=out_specs, check_vma=False)
```

```python
import functools
import itertools
import math

import jax
import jax.numpy as jnp
import numpy as np
from jax import lax
from jax.experimental import pallas as pl
from jax.experimental.pallas import tpu as pltpu
from jax.sharding import PartitionSpec as P

HEAD_DIM = 128
norm_eps = 1e-06
masked_score = -1e30
lanes = 128
mode_group = 8
seq_far = 2
head_batch = 8
vector_rows = 4
row_tile = 16
chunk_rows = row_tile


def mixer_tables(rate_now, angle_now, coef_now, skip_now, vectors):
    magnitude = jnp.exp(-rate_now)
    turn_re = magnitude * jnp.cos(angle_now)
    turn_im = magnitude * jnp.sin(angle_now)
    pole_sum = 2.0 * turn_re
    pole_product = -(magnitude * magnitude)
    direct = 2.0 * coef_now[0]
    delayed = -2.0 * (coef_now[0] * turn_re + coef_now[1] * turn_im)
    through = jnp.broadcast_to(skip_now, vectors.shape)
    halves = jnp.stack([
        jnp.concatenate([pole_sum, pole_product, through]),
        jnp.concatenate([direct, delayed, vectors]),
    ])
    return halves.reshape(halves.shape[:2] + (-1, lanes))


def inverse_rms(values):
    return lax.rsqrt(jnp.mean(values * values, axis=1, keepdims=True) + norm_eps)


def fetch(sources, targets, arrived):
    copies = [
        pltpu.make_async_copy(source, target, arrived.at[index])
        for index, (source, target) in enumerate(zip(sources, targets))
    ]
    for copy in copies:
        copy.start()
    return copies


def times(rows, weights):
    return jnp.dot(rows, weights, preferred_element_type=jnp.float32)


def add_projection(place_ref, out_ref, middle_ref, attended_ref, wholes, halves, copies):
    pipe, core = place_ref[0], place_ref[1]
    quarter = wholes.shape[2]

    def put(index, total):
        where = pl.ds(pl.multiple_of(index * quarter, lanes), quarter)
        out_ref[:, where] = (middle_ref[:, where].astype(jnp.float32) + total).astype(jnp.bfloat16)

    for index, hops in zip(range(wholes.shape[0]), (0, 1 + core, 2 - core, 3)):
        copies[index].wait()
        put(pipe ^ hops, times(attended_ref[...], wholes[index]))
    if halves is None:
        return
    half = halves.shape[1]
    total = 0.0
    for index, first in enumerate((core * half, (1 - core) * half)):
        copies[3 + index].wait()
        rows = attended_ref[:, pl.ds(pl.multiple_of(first, lanes), half)]
        total = total + times(rows, halves[index])
    put(pipe ^ 3, total)


def mix_attend(
    keep_ref, broken_ref, doc_col_ref, doc_row_ref, x_ref, pole_ref, zero_ref, middle_ref,
    attended_refs, signal, mixed, queries, keys, with_halo, after_middle, after_half,
):
    rows, width = x_ref.shape
    own = rows // 2
    folds = width // lanes
    modes = (pole_ref.shape[0] - vector_rows) // 2
    heads = width // HEAD_DIM
    tiles = rows // row_tile
    first_chunk = broken_ref[rows // chunk_rows]
    first_tile = first_chunk // 2 * 2

    @pl.when(first_chunk > first_tile)
    def _():
        blank = pl.ds(pl.multiple_of(first_tile * row_tile * folds, row_tile * folds), row_tile * folds)
        mixed[blank, :] = jnp.zeros((row_tile * folds, lanes), jnp.float32)

    def gain(row, fold):
        return zero_ref[2 * modes + row, fold : fold + 1, :]

    def in_pairs(body, first, last):
        def pair(index, carry):
            return body(2 * index + 1, body(2 * index, carry))

        lax.fori_loop(first // 2, last // 2, pair, 0)

    def spread(tile, carry):
        first = pl.multiple_of(tile * row_tile, row_tile)
        plain = x_ref[pl.ds(first, row_tile), :].astype(jnp.float32)
        scaled = plain * inverse_rms(plain)
        for fold in range(folds):
            where = pl.ds(first * folds + fold, row_tile, stride=folds)
            signal[where, :] = scaled[:, fold * lanes : (fold + 1) * lanes] * gain(0, fold)
        return carry

    in_pairs(spread, first_tile, tiles)

    def run_modes(group, opening):
        first_mode = group * mode_group
        coefs = [
            [
                ref[kind * modes + first_mode + index]
                for ref in (pole_ref, zero_ref)
                for kind in range(2)
            ]
            for index in range(mode_group)
        ]
        through = pole_ref[2 * modes] if opening else None

        def advance(chunk, state):
            def steps(state, masked):
                state = list(state)
                for step in range(chunk_rows):
                    row = chunk * chunk_rows + step
                    where = pl.ds(pl.multiple_of(row * folds, folds), folds)
                    entering = signal[where, :]
                    total = through * entering if opening else mixed[where, :]
                    for index in range(mode_group):
                        a1, a2, b0, b1 = coefs[index]
                        newer, older = state[2 * index], state[2 * index + 1]
                        if masked:
                            keep = keep_ref[row]
                            newer, older = newer * keep, older * keep
                        now = (entering + a2 * older) + a1 * newer
                        total = total + (b0 * now + b1 * newer)
                        state[2 * index], state[2 * index + 1] = now, newer
                    mixed[where, :] = total
                return tuple(state)

            return lax.cond(
                broken_ref[chunk] > 0,
                lambda held: steps(held, True),
                lambda held: steps(held, False),
                state,
            )

        zeros = jnp.zeros((folds, lanes), jnp.float32)
        lax.fori_loop(first_chunk, rows // chunk_rows, advance, (zeros,) * (2 * mode_group))

    run_modes(0, True)

    def later_modes(group, carry):
        run_modes(group, False)
        return carry

    lax.fori_loop(1, modes // mode_group, later_modes, 0)

    def gather_back(tile, carry):
        first = pl.multiple_of(tile * row_tile, row_tile)
        where_rows = pl.ds(first, row_tile)
        parts = [
            mixed[pl.ds(first * folds + fold, row_tile, stride=folds), :] for fold in range(folds)
        ]
        plain = x_ref[where_rows, :].astype(jnp.float32)
        middle = (plain + jnp.concatenate(parts, axis=1)).astype(jnp.bfloat16)
        middle_ref[where_rows, :] = middle
        wide = middle.astype(jnp.float32)
        normed = wide * inverse_rms(wide)
        for fold in range(folds):
            part = slice(fold * lanes, (fold + 1) * lanes)
            queries[where_rows, part] = (normed[:, part] * gain(1, fold)).astype(jnp.bfloat16)
            keys[where_rows, part] = (normed[:, part] * gain(2, fold)).astype(jnp.bfloat16)
        return carry

    def clear(tile, carry):
        first = pl.multiple_of(tile * row_tile, row_tile)
        for ref in (middle_ref, queries, keys):
            ref[pl.ds(first, row_tile), :] = jnp.zeros((row_tile, width), jnp.bfloat16)
        return carry

    in_pairs(clear, 0, first_tile)
    in_pairs(gather_back, first_tile, tiles)
    after_middle()

    query_pos = lax.broadcasted_iota(jnp.int32, (own, rows), 0) + own
    key_pos = lax.broadcasted_iota(jnp.int32, (own, rows), 1)
    allowed_own = (key_pos <= query_pos) & (doc_col_ref[own:, :] == doc_row_ref[...])
    allowed_halo = (key_pos[:, :own] <= query_pos[:, :own] - own) & (
        doc_col_ref[:own, :] == doc_row_ref[:, :own]
    )
    rate = HEAD_DIM ** (-0.5) * math.log2(math.e)
    blocks = [(own, rows, allowed_own)]
    if with_halo:
        blocks.insert(0, (0, own, allowed_halo))
    skipped = rows - own * len(blocks)
    for batch in range(0, heads, head_batch):
        jobs = [
            (head, first, count, allowed)
            for head in range(batch, batch + head_batch)
            for first, count, allowed in blocks
        ]
        raws = []
        for head, first, count, allowed in jobs:
            where = slice(head * HEAD_DIM, (head + 1) * HEAD_DIM)
            scores = lax.dot_general(
                queries[first : first + own, where], keys[:count, where], (((1,), (1,)), ((), ())),
                preferred_element_type=jnp.float32,
            )
            raws.append(jnp.where(allowed, scores, masked_score))
        tops = [jnp.max(raw, axis=1, keepdims=True) for raw in raws]
        raws = [jnp.exp2((raw - top) * rate) for raw, top in zip(raws, tops)]
        sums = [jnp.sum(raw, axis=1, keepdims=True) for raw in raws]
        raws = [(raw * (1.0 / total)).astype(jnp.bfloat16) for raw, total in zip(raws, sums)]
        for (head, first, count, _), weights in zip(jobs, raws):
            where = slice(head * HEAD_DIM, (head + 1) * HEAD_DIM)
            part, inner = divmod(head, heads // 2)
            placed = slice(inner * HEAD_DIM, (inner + 1) * HEAD_DIM)
            attended_refs[part][first - skipped : first - skipped + own, placed] = times(
                weights, middle_ref[:count, where]
            ).astype(jnp.bfloat16)
        if (batch + head_batch) % (heads // 2) == 0:
            after_half(batch // (heads // 2))


def section_kernel(wholes_count, halves_count, mixes, with_halo, *refs):
    refs = list(refs)

    def take(count):
        taken, refs[:count] = refs[:count], []
        return taken

    place_ref, = take(1)
    if mixes:
        keep_ref, broken_ref, doc_col_ref, doc_row_ref, tables_ref = take(5)
    sources, weights = take(2), take(wholes_count + halves_count)
    if mixes:
        middle_out, attended_out = take(2)
    else:
        out_ref, = take(1)
    arrived, = take(1)
    if mixes:
        x_ref, pole_ref, zero_ref, middle_ref, low_ref, high_ref, signal, mixed, queries, keys = take(10)
        copies = fetch(
            [tables_ref.at[place_ref[2]], tables_ref.at[place_ref[3]]], [pole_ref, zero_ref],
            arrived.at[pl.ds(10, 2)],
        )
    if weights:
        middle_in, attended_in, wholes = take(3)
        halves = take(1)[0] if halves_count else None
        skipped = sources[0].shape[0] - middle_in.shape[0]
        rows = pl.ds(skipped, middle_in.shape[0])
        inputs = fetch([source.at[rows] for source in sources], [middle_in, attended_in], arrived)
        targets = [wholes.at[index] for index in range(wholes_count)]
        targets += [halves.at[index] for index in range(halves_count)]
        pieces = fetch(weights, targets, arrived.at[pl.ds(2, 5)])
        for copy in inputs:
            copy.wait()
        target = x_ref if mixes else out_ref
        add_projection(place_ref, target, middle_in, attended_in, wholes, halves, pieces)
    else:
        own = x_ref.shape[0] // 2
        inputs = fetch(sources, [x_ref.at[pl.ds(0, own)], x_ref.at[pl.ds(own, own)]], arrived)
        for copy in inputs:
            copy.wait()
    if not mixes:
        return
    for copy in copies:
        copy.wait()
    skipped = middle_ref.shape[0] - middle_out.shape[0]
    half = low_ref.shape[1]
    results = [
        pltpu.make_async_copy(
            middle_ref.at[pl.ds(skipped, middle_out.shape[0])], middle_out, arrived.at[7]
        )
    ] + [
        pltpu.make_async_copy(
            ref, attended_out.at[:, pl.ds(index * half, half)], arrived.at[8 + index]
        )
        for index, ref in enumerate((low_ref, high_ref))
    ]
    mix_attend(
        keep_ref, broken_ref, doc_col_ref, doc_row_ref, x_ref, pole_ref, zero_ref, middle_ref,
        (low_ref, high_ref), signal, mixed, queries, keys, with_halo,
        results[0].start, lambda part: results[1 + part].start(),
    )
    for copy in results:
        copy.wait()


def section_step(place, sources, weights=(), mixing=(), with_halo=True):
    width = sources[0].shape[1]
    smem, vmem, anywhere = (
        pl.BlockSpec(memory_space=space) for space in (pltpu.SMEM, pltpu.VMEM, pltpu.HBM)
    )
    rows = sources[0].shape[0] if weights else 2 * sources[0].shape[0]
    folds = width // lanes
    wholes_count = sum(weight.shape[0] == width for weight in weights)
    halves_count = len(weights) - wholes_count
    scratch = [pltpu.SemaphoreType.DMA((12,))]
    if mixing:
        kept = rows if with_halo else rows // 2
        wide = pltpu.VMEM((rows * folds, lanes), jnp.float32)
        narrow = pltpu.VMEM((rows, width), jnp.bfloat16)
        half = pltpu.VMEM((kept, width // 2), jnp.bfloat16)
        table = pltpu.VMEM(mixing[-1].shape[1:], jnp.float32)
        scratch += [narrow, table, table, narrow, half, half, wide, wide, narrow, narrow]
        out_shape = [jax.ShapeDtypeStruct((kept, width), jnp.bfloat16)] * 2
        out_specs = [anywhere, anywhere]
    else:
        kept = rows
        out_shape = jax.ShapeDtypeStruct((rows, width), jnp.bfloat16)
        out_specs = vmem
    if weights:
        held = pltpu.VMEM((rows, width), jnp.bfloat16)
        scratch += [
            held, held,
            pltpu.VMEM((wholes_count,) + weights[0].shape, jnp.bfloat16),
        ]
        if halves_count:
            scratch.append(pltpu.VMEM((halves_count,) + weights[-1].shape, jnp.bfloat16))
    return pl.pallas_call(
        functools.partial(section_kernel, wholes_count, halves_count, bool(mixing), with_halo),
        out_shape=out_shape,
        in_specs=[smem]
        + ([smem, smem, vmem, vmem, anywhere] if mixing else [])
        + [anywhere] * (len(sources) + len(weights)),
        out_specs=out_specs,
        scratch_shapes=scratch,
        compiler_params=pltpu.CompilerParams(vmem_limit_bytes=60 << 20),
        cost_estimate=pl.CostEstimate(
            flops=2 * rows * width * width, bytes_accessed=2 * width * width, transcendentals=0
        ),
        name="section_step",
    )(place, *mixing, *sources, *weights)


def half_copy_kernel(place_ref, value_ref, out_ref, held, arrived, left):
    half = out_ref.shape[0]
    part = half // 4
    parts = [pl.ds(index * part, part) for index in range(4)]
    starts = [place_ref[1] * half + index * part for index in range(4)]
    sources = [value_ref.at[pl.ds(first, part)] for first in starts]
    coming = fetch(sources, [held.at[where] for where in parts], arrived)
    going = []
    for index, where in enumerate(parts):
        coming[index].wait()
        going.append(pltpu.make_async_copy(held.at[where], out_ref.at[where], left.at[index]))
        going[-1].start()
    for copy in going:
        copy.wait()


def core_half(value, place):
    hbm = pl.BlockSpec(memory_space=pltpu.HBM)
    shape = (value.shape[0] // 2,) + value.shape[1:]
    return pl.pallas_call(
        half_copy_kernel,
        out_shape=jax.ShapeDtypeStruct(shape, value.dtype),
        in_specs=[pl.BlockSpec(memory_space=pltpu.SMEM), hbm],
        out_specs=hbm,
        scratch_shapes=[pltpu.VMEM(shape, value.dtype)] + [pltpu.SemaphoreType.DMA((4,))] * 2,
        compiler_params=pltpu.CompilerParams(vmem_limit_bytes=60 << 20),
        name="core_half",
    )(place, value)


def document_flags(docs):
    goes_on = jnp.concatenate([jnp.zeros((1,), bool), docs[1:] == docs[:-1]])
    broken = jnp.any(jnp.logical_not(goes_on).reshape(-1, chunk_rows), axis=1)
    needed = docs == docs[docs.shape[0] // 2]
    first_chunk = jnp.argmax(needed) // chunk_rows
    flags = jnp.concatenate([broken.astype(jnp.int32), first_chunk.astype(jnp.int32)[None]])
    return goes_on.astype(jnp.float32), flags


def across(value, hops):
    count = lax.axis_size("pipe")
    return lax.ppermute(value, "pipe", [(i, i ^ hops) for i in range(count)])


def swapped(value):
    count = lax.axis_size("seq")
    return lax.ppermute(value, "seq", [(i, i ^ 1) for i in range(count)])


def spread_quarters(shard, offset, first):
    section_count = lax.axis_size("pipe")
    pipe_index = lax.axis_index("pipe")
    quarter = shard.shape[1] // section_count

    def columns(hops):
        return lax.dynamic_slice_in_dim(shard, (pipe_index ^ hops ^ offset) * quarter, quarter, 1)

    held = [columns(0)]
    for hops in range(1, section_count):
        pairs = [(i, i ^ hops) for i in range(first, section_count)]
        held.append(lax.ppermute(columns(hops), "pipe", pairs))
    held = jnp.stack(held)
    return {
        section: lax.dynamic_index_in_dim(held, pipe_index ^ section, 0, False)
        for section in range(first, section_count)
    }


def own_half(halves):
    return lax.dynamic_index_in_dim(halves, lax.axis_index("seq") % 2, 0, False)


def joined_tables(halves, fetched):
    fetched = jnp.stack(fetched)
    other = swapped(fetched)
    own = jnp.where(lax.axis_index("seq") % 2 == 0, halves, halves[::-1])
    return jnp.concatenate([own, jnp.stack([fetched, other], axis=1).reshape((-1,) + own.shape[1:])])


def sent_by_core(value, hops_by_core):
    pipe_count, seq_count = lax.axis_size("pipe"), lax.axis_size("seq")
    pairs = [
        (pipe * seq_count + seq, (pipe ^ hops_by_core[seq % 2]) * seq_count + seq)
        for pipe in range(pipe_count)
        for seq in range(seq_count)
    ]
    return lax.ppermute(value, ("pipe", "seq"), pairs)


def passed_on(fetched, place):
    return sent_by_core(core_half(fetched, place), (2, 1))


def permuted_rows(value, order):
    count = lax.axis_size("pipe")
    choices = list(itertools.permutations(range(count)))
    match = jnp.all(jnp.asarray(np.array(choices, np.int32)) == order[None, :], axis=1)
    which = jnp.argmax(match).astype(jnp.int32)

    def mover(choice):
        pairs = [(source, target) for target, source in enumerate(choice)]
        return lambda held: lax.ppermute(held, "pipe", pairs)

    return lax.switch(which, [mover(choice) for choice in choices], value)


def local(inputs, lengths, order, norm_gain, rate, angle, coef, skip, score_gains, out_proj):
    section_count = lax.axis_size("pipe")
    seq_count = lax.axis_size("seq")
    pipe_index = lax.axis_index("pipe")
    seq_index = lax.axis_index("seq")
    row_count = inputs.shape[1]

    place = jnp.stack([pipe_index, seq_index % 2]).astype(jnp.int32)
    vectors = jnp.concatenate([norm_gain, score_gains[0], skip])
    halves = mixer_tables(rate[0], angle[0], coef[0], skip[0], vectors)

    tie = lax.optimization_barrier
    quarters = spread_quarters(out_proj[0], 0, 0)
    held = (quarters, halves, inputs[0], out_proj[0])
    quarters, halves, entering, shard = tie(held)

    def along_seq(quarters):
        return {
            section: lax.all_gather(quarter, "seq", axis=0, tiled=True)
            for section, quarter in quarters.items()
        }

    wholes = along_seq({0: quarters.pop(0)})
    held = (permuted_rows(entering, order), halves, shard, quarters)
    own, halves, shard, quarters = tie(held)
    wholes.update(along_seq(quarters))
    fetched = [across(own_half(halves), hops) for hops in range(1, section_count)]
    last_quarters = spread_quarters(shard, 3, seq_far)
    before = lax.ppermute(own, "seq", [(i, i + 1) for i in range(seq_count - 1)])

    positions = (seq_index - 1) * row_count + jnp.arange(2 * row_count)
    chosen = lax.dynamic_index_in_dim(order, pipe_index, 0, False)
    doc_ends = jnp.cumsum(lax.dynamic_index_in_dim(lengths, chosen, 0, False))
    counted = jnp.sum((doc_ends[None, :] <= positions[:, None]).astype(jnp.int32), axis=1)
    docs = jnp.where(positions >= 0, counted, -1)
    keep, flags = document_flags(docs)

    def hop(section):
        return sent_by_core(wholes[section], (1, 2))

    def mixing(section):
        hops = 2 * (pipe_index ^ section)
        which = jnp.stack([hops + place[1], hops + 1 - place[1]])
        return jnp.concatenate([place, which]), (keep, flags, docs[:, None], docs[None, :], tables)

    near, far = {}, {}
    fetched, wholes[0] = tie((fetched, wholes[0]))
    near[0] = hop(0)
    held = (near[0], wholes[1], own, before, fetched, last_quarters)
    near[0], wholes[1], own, before, fetched, last_quarters = tie(held)
    half = core_half(near[0], place)
    half, own, before, fetched, halves = tie((half, own, before, fetched, halves))
    far[0] = sent_by_core(half, (2, 1))
    near[1] = hop(1)
    last_quarters = along_seq(last_quarters)
    tables = joined_tables(halves, fetched)
    where, mixer = mixing(0)
    middle, attended = section_step(where, (before, own), mixing=mixer)
    for section in range(section_count):
        weights = [wholes[section], near[section], swapped(near[section])]
        if section < seq_far:
            far[section], middle, attended = tie((far[section], middle, attended))
            weights += [far[section], swapped(far[section])]
        else:
            weights += [last_quarters[section]]
        if section + 2 < section_count:
            wholes[section + 2], middle, attended = tie((wholes[section + 2], middle, attended))
            near[section + 2] = hop(section + 2)
        if section + 1 < section_count:
            near[section + 1], middle, attended = tie((near[section + 1], middle, attended))
            if section + 1 < seq_far:
                far[section + 1] = passed_on(near[section + 1], place)
            where, mixer = mixing(section + 1)
            with_halo = section + 2 < section_count
            middle, attended = section_step(where, (middle, attended), weights, mixer, with_halo)
    x = section_step(place, (middle, attended), weights)
    return x[None]


def solution(mesh):
    in_specs = (
        P("pipe", "seq", None),
        P(),
        P(),
        P("pipe", None),
        P("pipe", None, None),
        P("pipe", None, None),
        P("pipe", None, None, None),
        P("pipe", None),
        P("pipe", None, None),
        P("pipe", "seq", None),
    )
    out_specs = P("pipe", "seq", None)
    return jax.shard_map(local, mesh=mesh, in_specs=in_specs, out_specs=out_specs, check_vma=False)
```

```python
import functools
import itertools
import math

import jax
import jax.numpy as jnp
import numpy as np
from jax import lax
from jax.experimental import pallas as pl
from jax.experimental.pallas import tpu as pltpu
from jax.sharding import PartitionSpec as P

HEAD_DIM = 128
norm_eps = 1e-06
masked_score = -1e30
lanes = 128
mode_group = 8
seq_far = 2
head_batch = 8
vector_rows = 4
row_tile = 16
chunk_rows = row_tile


def mixer_tables(rate_now, angle_now, coef_now, skip_now, vectors):
    magnitude = jnp.exp(-rate_now)
    turn_re = magnitude * jnp.cos(angle_now)
    turn_im = magnitude * jnp.sin(angle_now)
    pole_sum = 2.0 * turn_re
    pole_product = -(magnitude * magnitude)
    direct = 2.0 * coef_now[0]
    delayed = -2.0 * (coef_now[0] * turn_re + coef_now[1] * turn_im)
    through = jnp.broadcast_to(skip_now, vectors.shape)
    halves = jnp.stack([
        jnp.concatenate([pole_sum, pole_product, through]),
        jnp.concatenate([direct, delayed, vectors]),
    ])
    return halves.reshape(halves.shape[:2] + (-1, lanes))


def inverse_rms(values):
    return lax.rsqrt(jnp.mean(values * values, axis=1, keepdims=True) + norm_eps)


def fetch(sources, targets, arrived):
    copies = [
        pltpu.make_async_copy(source, target, arrived.at[index])
        for index, (source, target) in enumerate(zip(sources, targets))
    ]
    for copy in copies:
        copy.start()
    return copies


def times(rows, weights):
    return jnp.dot(rows, weights, preferred_element_type=jnp.float32)


def add_projection(place_ref, out_ref, middle_ref, attended_ref, wholes, halves, copies):
    pipe, core = place_ref[0], place_ref[1]
    quarter = wholes.shape[2]

    def put(index, total):
        where = pl.ds(pl.multiple_of(index * quarter, lanes), quarter)
        out_ref[:, where] = (middle_ref[:, where].astype(jnp.float32) + total).astype(jnp.bfloat16)

    for index, hops in zip(range(wholes.shape[0]), (0, 1 + core, 2 - core, 3)):
        copies[index].wait()
        put(pipe ^ hops, times(attended_ref[...], wholes[index]))
    if halves is None:
        return
    half = halves.shape[1]
    total = 0.0
    for index, first in enumerate((core * half, (1 - core) * half)):
        copies[3 + index].wait()
        rows = attended_ref[:, pl.ds(pl.multiple_of(first, lanes), half)]
        total = total + times(rows, halves[index])
    put(pipe ^ 3, total)


def mix_attend(
    keep_ref, broken_ref, doc_col_ref, doc_row_ref, x_ref, pole_ref, zero_ref, middle_ref,
    attended_refs, signal, mixed, queries, keys, with_halo, after_middle, after_half,
):
    rows, width = x_ref.shape
    own = rows // 2
    folds = width // lanes
    modes = (pole_ref.shape[0] - vector_rows) // 2
    heads = width // HEAD_DIM
    tiles = rows // row_tile
    first_chunk = broken_ref[rows // chunk_rows]
    first_tile = first_chunk // 2 * 2

    @pl.when(first_chunk > first_tile)
    def _():
        blank = pl.ds(pl.multiple_of(first_tile * row_tile * folds, row_tile * folds), row_tile * folds)
        mixed[blank, :] = jnp.zeros((row_tile * folds, lanes), jnp.float32)

    def gain(row, fold):
        return zero_ref[2 * modes + row, fold : fold + 1, :]

    def in_pairs(body, first, last):
        def pair(index, carry):
            return body(2 * index + 1, body(2 * index, carry))

        lax.fori_loop(first // 2, last // 2, pair, 0)

    def spread(tile, carry):
        first = pl.multiple_of(tile * row_tile, row_tile)
        plain = x_ref[pl.ds(first, row_tile), :].astype(jnp.float32)
        scaled = plain * inverse_rms(plain)
        for fold in range(folds):
            where = pl.ds(first * folds + fold, row_tile, stride=folds)
            signal[where, :] = scaled[:, fold * lanes : (fold + 1) * lanes] * gain(0, fold)
        return carry

    in_pairs(spread, first_tile, tiles)

    def run_modes(group, opening):
        first_mode = group * mode_group
        coefs = [
            [
                ref[kind * modes + first_mode + index]
                for ref in (pole_ref, zero_ref)
                for kind in range(2)
            ]
            for index in range(mode_group)
        ]
        through = pole_ref[2 * modes] if opening else None

        def advance(chunk, state):
            def steps(state, masked):
                state = list(state)
                for step in range(chunk_rows):
                    row = chunk * chunk_rows + step
                    where = pl.ds(pl.multiple_of(row * folds, folds), folds)
                    entering = signal[where, :]
                    total = through * entering if opening else mixed[where, :]
                    for index in range(mode_group):
                        a1, a2, b0, b1 = coefs[index]
                        newer, older = state[2 * index], state[2 * index + 1]
                        if masked:
                            keep = keep_ref[row]
                            newer, older = newer * keep, older * keep
                        now = (entering + a2 * older) + a1 * newer
                        total = total + (b0 * now + b1 * newer)
                        state[2 * index], state[2 * index + 1] = now, newer
                    mixed[where, :] = total
                return tuple(state)

            return lax.cond(
                broken_ref[chunk] > 0,
                lambda held: steps(held, True),
                lambda held: steps(held, False),
                state,
            )

        zeros = jnp.zeros((folds, lanes), jnp.float32)
        lax.fori_loop(first_chunk, rows // chunk_rows, advance, (zeros,) * (2 * mode_group))

    run_modes(0, True)

    def later_modes(group, carry):
        run_modes(group, False)
        return carry

    lax.fori_loop(1, modes // mode_group, later_modes, 0)

    def gather_back(tile, carry):
        first = pl.multiple_of(tile * row_tile, row_tile)
        where_rows = pl.ds(first, row_tile)
        parts = [
            mixed[pl.ds(first * folds + fold, row_tile, stride=folds), :] for fold in range(folds)
        ]
        plain = x_ref[where_rows, :].astype(jnp.float32)
        middle = (plain + jnp.concatenate(parts, axis=1)).astype(jnp.bfloat16)
        middle_ref[where_rows, :] = middle
        wide = middle.astype(jnp.float32)
        normed = wide * inverse_rms(wide)
        for fold in range(folds):
            part = slice(fold * lanes, (fold + 1) * lanes)
            queries[where_rows, part] = (normed[:, part] * gain(1, fold)).astype(jnp.bfloat16)
            keys[where_rows, part] = (normed[:, part] * gain(2, fold)).astype(jnp.bfloat16)
        return carry

    def clear(tile, carry):
        first = pl.multiple_of(tile * row_tile, row_tile)
        for ref in (middle_ref, queries, keys):
            ref[pl.ds(first, row_tile), :] = jnp.zeros((row_tile, width), jnp.bfloat16)
        return carry

    in_pairs(clear, 0, first_tile)
    in_pairs(gather_back, first_tile, tiles)
    after_middle()

    query_pos = lax.broadcasted_iota(jnp.int32, (own, rows), 0) + own
    key_pos = lax.broadcasted_iota(jnp.int32, (own, rows), 1)
    allowed_own = (key_pos <= query_pos) & (doc_col_ref[own:, :] == doc_row_ref[...])
    allowed_halo = (key_pos[:, :own] <= query_pos[:, :own] - own) & (
        doc_col_ref[:own, :] == doc_row_ref[:, :own]
    )
    rate = HEAD_DIM ** (-0.5) * math.log2(math.e)
    blocks = [(own, rows, allowed_own)]
    if with_halo:
        blocks.insert(0, (0, own, allowed_halo))
    skipped = rows - own * len(blocks)
    for batch in range(0, heads, head_batch):
        jobs = [
            (head, first, count, allowed)
            for head in range(batch, batch + head_batch)
            for first, count, allowed in blocks
        ]
        raws = []
        for head, first, count, allowed in jobs:
            where = slice(head * HEAD_DIM, (head + 1) * HEAD_DIM)
            scores = lax.dot_general(
                queries[first : first + own, where], keys[:count, where], (((1,), (1,)), ((), ())),
                preferred_element_type=jnp.float32,
            )
            raws.append(jnp.where(allowed, scores, masked_score))
        tops = [jnp.max(raw, axis=1, keepdims=True) for raw in raws]
        raws = [jnp.exp2((raw - top) * rate) for raw, top in zip(raws, tops)]
        sums = [jnp.sum(raw, axis=1, keepdims=True) for raw in raws]
        raws = [(raw * (1.0 / total)).astype(jnp.bfloat16) for raw, total in zip(raws, sums)]
        for (head, first, count, _), weights in zip(jobs, raws):
            where = slice(head * HEAD_DIM, (head + 1) * HEAD_DIM)
            part, inner = divmod(head, heads // 2)
            placed = slice(inner * HEAD_DIM, (inner + 1) * HEAD_DIM)
            attended_refs[part][first - skipped : first - skipped + own, placed] = times(
                weights, middle_ref[:count, where]
            ).astype(jnp.bfloat16)
        if (batch + head_batch) % (heads // 2) == 0:
            after_half(batch // (heads // 2))


def section_kernel(wholes_count, halves_count, mixes, with_halo, *refs):
    refs = list(refs)

    def take(count):
        taken, refs[:count] = refs[:count], []
        return taken

    place_ref, = take(1)
    if mixes:
        keep_ref, broken_ref, doc_col_ref, doc_row_ref, tables_ref = take(5)
    sources, weights = take(2), take(wholes_count + halves_count)
    if mixes:
        middle_out, attended_out = take(2)
    else:
        out_ref, = take(1)
    arrived, = take(1)
    if mixes:
        x_ref, pole_ref, zero_ref, middle_ref, low_ref, high_ref, signal, mixed, queries, keys = take(10)
        copies = fetch(
            [tables_ref.at[place_ref[2]], tables_ref.at[place_ref[3]]], [pole_ref, zero_ref],
            arrived.at[pl.ds(10, 2)],
        )
    if weights:
        middle_in, attended_in, wholes = take(3)
        halves = take(1)[0] if halves_count else None
        skipped = sources[0].shape[0] - middle_in.shape[0]
        rows = pl.ds(skipped, middle_in.shape[0])
        inputs = fetch([source.at[rows] for source in sources], [middle_in, attended_in], arrived)
        targets = [wholes.at[index] for index in range(wholes_count)]
        targets += [halves.at[index] for index in range(halves_count)]
        pieces = fetch(weights, targets, arrived.at[pl.ds(2, 5)])
        for copy in inputs:
            copy.wait()
        target = x_ref if mixes else out_ref
        add_projection(place_ref, target, middle_in, attended_in, wholes, halves, pieces)
    else:
        own = x_ref.shape[0] // 2
        inputs = fetch(sources, [x_ref.at[pl.ds(0, own)], x_ref.at[pl.ds(own, own)]], arrived)
        for copy in inputs:
            copy.wait()
    if not mixes:
        return
    for copy in copies:
        copy.wait()
    skipped = middle_ref.shape[0] - middle_out.shape[0]
    half = low_ref.shape[1]
    results = [
        pltpu.make_async_copy(
            middle_ref.at[pl.ds(skipped, middle_out.shape[0])], middle_out, arrived.at[7]
        )
    ] + [
        pltpu.make_async_copy(
            ref, attended_out.at[:, pl.ds(index * half, half)], arrived.at[8 + index]
        )
        for index, ref in enumerate((low_ref, high_ref))
    ]
    mix_attend(
        keep_ref, broken_ref, doc_col_ref, doc_row_ref, x_ref, pole_ref, zero_ref, middle_ref,
        (low_ref, high_ref), signal, mixed, queries, keys, with_halo,
        results[0].start, lambda part: results[1 + part].start(),
    )
    for copy in results:
        copy.wait()


def section_step(place, sources, weights=(), mixing=(), with_halo=True):
    width = sources[0].shape[1]
    smem, vmem, anywhere = (
        pl.BlockSpec(memory_space=space) for space in (pltpu.SMEM, pltpu.VMEM, pltpu.HBM)
    )
    rows = sources[0].shape[0] if weights else 2 * sources[0].shape[0]
    folds = width // lanes
    wholes_count = sum(weight.shape[0] == width for weight in weights)
    halves_count = len(weights) - wholes_count
    scratch = [pltpu.SemaphoreType.DMA((12,))]
    if mixing:
        kept = rows if with_halo else rows // 2
        wide = pltpu.VMEM((rows * folds, lanes), jnp.float32)
        narrow = pltpu.VMEM((rows, width), jnp.bfloat16)
        half = pltpu.VMEM((kept, width // 2), jnp.bfloat16)
        table = pltpu.VMEM(mixing[-1].shape[1:], jnp.float32)
        scratch += [narrow, table, table, narrow, half, half, wide, wide, narrow, narrow]
        out_shape = [jax.ShapeDtypeStruct((kept, width), jnp.bfloat16)] * 2
        out_specs = [anywhere, anywhere]
    else:
        kept = rows
        out_shape = jax.ShapeDtypeStruct((rows, width), jnp.bfloat16)
        out_specs = vmem
    if weights:
        held = pltpu.VMEM((rows, width), jnp.bfloat16)
        scratch += [
            held, held,
            pltpu.VMEM((wholes_count,) + weights[0].shape, jnp.bfloat16),
        ]
        if halves_count:
            scratch.append(pltpu.VMEM((halves_count,) + weights[-1].shape, jnp.bfloat16))
    return pl.pallas_call(
        functools.partial(section_kernel, wholes_count, halves_count, bool(mixing), with_halo),
        out_shape=out_shape,
        in_specs=[smem]
        + ([smem, smem, vmem, vmem, anywhere] if mixing else [])
        + [anywhere] * (len(sources) + len(weights)),
        out_specs=out_specs,
        scratch_shapes=scratch,
        compiler_params=pltpu.CompilerParams(vmem_limit_bytes=60 << 20),
        cost_estimate=pl.CostEstimate(
            flops=2 * rows * width * width, bytes_accessed=2 * width * width, transcendentals=0
        ),
        name="section_step",
    )(place, *mixing, *sources, *weights)


def half_copy_kernel(place_ref, value_ref, out_ref, held, arrived, left):
    half = out_ref.shape[0]
    part = half // 4
    parts = [pl.ds(index * part, part) for index in range(4)]
    starts = [place_ref[1] * half + index * part for index in range(4)]
    sources = [value_ref.at[pl.ds(first, part)] for first in starts]
    coming = fetch(sources, [held.at[where] for where in parts], arrived)
    going = []
    for index, where in enumerate(parts):
        coming[index].wait()
        going.append(pltpu.make_async_copy(held.at[where], out_ref.at[where], left.at[index]))
        going[-1].start()
    for copy in going:
        copy.wait()


def core_half(value, place):
    hbm = pl.BlockSpec(memory_space=pltpu.HBM)
    shape = (value.shape[0] // 2,) + value.shape[1:]
    return pl.pallas_call(
        half_copy_kernel,
        out_shape=jax.ShapeDtypeStruct(shape, value.dtype),
        in_specs=[pl.BlockSpec(memory_space=pltpu.SMEM), hbm],
        out_specs=hbm,
        scratch_shapes=[pltpu.VMEM(shape, value.dtype)] + [pltpu.SemaphoreType.DMA((4,))] * 2,
        compiler_params=pltpu.CompilerParams(vmem_limit_bytes=60 << 20),
        name="core_half",
    )(place, value)


def document_flags(docs):
    goes_on = jnp.concatenate([jnp.zeros((1,), bool), docs[1:] == docs[:-1]])
    broken = jnp.any(jnp.logical_not(goes_on).reshape(-1, chunk_rows), axis=1)
    needed = docs == docs[docs.shape[0] // 2]
    first_chunk = jnp.argmax(needed) // chunk_rows
    flags = jnp.concatenate([broken.astype(jnp.int32), first_chunk.astype(jnp.int32)[None]])
    return goes_on.astype(jnp.float32), flags


def across(value, hops):
    count = lax.axis_size("pipe")
    return lax.ppermute(value, "pipe", [(i, i ^ hops) for i in range(count)])


def swapped(value):
    count = lax.axis_size("seq")
    return lax.ppermute(value, "seq", [(i, i ^ 1) for i in range(count)])


def spread_quarters(shard, offset, first):
    section_count = lax.axis_size("pipe")
    pipe_index = lax.axis_index("pipe")
    quarter = shard.shape[1] // section_count

    def columns(hops):
        return lax.dynamic_slice_in_dim(shard, (pipe_index ^ hops ^ offset) * quarter, quarter, 1)

    held = [columns(0)]
    for hops in range(1, section_count):
        pairs = [(i, i ^ hops) for i in range(first, section_count)]
        held.append(lax.ppermute(columns(hops), "pipe", pairs))
    held = jnp.stack(held)
    return {
        section: lax.dynamic_index_in_dim(held, pipe_index ^ section, 0, False)
        for section in range(first, section_count)
    }


def own_half(halves):
    return lax.dynamic_index_in_dim(halves, lax.axis_index("seq") % 2, 0, False)


def joined_tables(halves, fetched):
    fetched = jnp.stack(fetched)
    other = swapped(fetched)
    own = jnp.where(lax.axis_index("seq") % 2 == 0, halves, halves[::-1])
    return jnp.concatenate([own, jnp.stack([fetched, other], axis=1).reshape((-1,) + own.shape[1:])])


def sent_by_core(value, hops_by_core):
    pipe_count, seq_count = lax.axis_size("pipe"), lax.axis_size("seq")
    pairs = [
        (pipe * seq_count + seq, (pipe ^ hops_by_core[seq % 2]) * seq_count + seq)
        for pipe in range(pipe_count)
        for seq in range(seq_count)
    ]
    return lax.ppermute(value, ("pipe", "seq"), pairs)


def passed_on(fetched, place):
    return sent_by_core(core_half(fetched, place), (2, 1))


def permutation_index(order):
    choices = list(itertools.permutations(range(lax.axis_size("pipe"))))
    match = jnp.all(jnp.asarray(np.array(choices, np.int32)) == order[None, :], axis=1)
    return jnp.argmax(match).astype(jnp.int32)


def permuted_rows(value, which):
    choices = list(itertools.permutations(range(lax.axis_size("pipe"))))

    def mover(choice):
        pairs = [(source, target) for target, source in enumerate(choice)]
        return lambda held: lax.ppermute(held, "pipe", pairs)

    return lax.switch(which, [mover(choice) for choice in choices], value)


def local(inputs, lengths, order, norm_gain, rate, angle, coef, skip, score_gains, out_proj):
    section_count = lax.axis_size("pipe")
    seq_count = lax.axis_size("seq")
    pipe_index = lax.axis_index("pipe")
    seq_index = lax.axis_index("seq")
    row_count = inputs.shape[1]

    place = jnp.stack([pipe_index, seq_index % 2]).astype(jnp.int32)
    vectors = jnp.concatenate([norm_gain, score_gains[0], skip])
    halves = mixer_tables(rate[0], angle[0], coef[0], skip[0], vectors)

    tie = lax.optimization_barrier
    quarters = spread_quarters(out_proj[0], 0, 0)
    held = (quarters, halves, inputs[0], out_proj[0], permutation_index(order))
    quarters, halves, entering, shard, which = tie(held)

    def along_seq(quarters):
        return {
            section: lax.all_gather(quarter, "seq", axis=0, tiled=True)
            for section, quarter in quarters.items()
        }

    wholes = along_seq({0: quarters.pop(0)})
    held = (permuted_rows(entering, which), halves, shard, quarters)
    own, halves, shard, quarters = tie(held)
    wholes.update(along_seq(quarters))
    fetched = [across(own_half(halves), hops) for hops in range(1, section_count)]
    last_quarters = spread_quarters(shard, 3, seq_far)
    before = lax.ppermute(own, "seq", [(i, i + 1) for i in range(seq_count - 1)])

    positions = (seq_index - 1) * row_count + jnp.arange(2 * row_count)
    chosen = lax.dynamic_index_in_dim(order, pipe_index, 0, False)
    doc_ends = jnp.cumsum(lax.dynamic_index_in_dim(lengths, chosen, 0, False))
    counted = jnp.sum((doc_ends[None, :] <= positions[:, None]).astype(jnp.int32), axis=1)
    docs = jnp.where(positions >= 0, counted, -1)
    keep, flags = document_flags(docs)

    def hop(section):
        return sent_by_core(wholes[section], (1, 2))

    def mixing(section):
        hops = 2 * (pipe_index ^ section)
        which = jnp.stack([hops + place[1], hops + 1 - place[1]])
        return jnp.concatenate([place, which]), (keep, flags, docs[:, None], docs[None, :], tables)

    near, far = {}, {}
    fetched, wholes[0] = tie((fetched, wholes[0]))
    near[0] = hop(0)
    held = (near[0], wholes[1], own, before, fetched, last_quarters)
    near[0], wholes[1], own, before, fetched, last_quarters = tie(held)
    half = core_half(near[0], place)
    half, own, before, fetched, halves = tie((half, own, before, fetched, halves))
    far[0] = sent_by_core(half, (2, 1))
    near[1] = hop(1)
    last_quarters = along_seq(last_quarters)
    tables = joined_tables(halves, fetched)
    where, mixer = mixing(0)
    middle, attended = section_step(where, (before, own), mixing=mixer)
    for section in range(section_count):
        weights = [wholes[section], near[section], swapped(near[section])]
        if section < seq_far:
            far[section], middle, attended = tie((far[section], middle, attended))
            weights += [far[section], swapped(far[section])]
        else:
            weights += [last_quarters[section]]
        if section + 2 < section_count:
            wholes[section + 2], middle, attended = tie((wholes[section + 2], middle, attended))
            near[section + 2] = hop(section + 2)
        if section + 1 < section_count:
            near[section + 1], middle, attended = tie((near[section + 1], middle, attended))
            if section + 1 < seq_far:
                far[section + 1] = passed_on(near[section + 1], place)
            where, mixer = mixing(section + 1)
            with_halo = section + 2 < section_count
            middle, attended = section_step(where, (middle, attended), weights, mixer, with_halo)
    x = section_step(place, (middle, attended), weights)
    return x[None]


def solution(mesh):
    in_specs = (
        P("pipe", "seq", None),
        P(),
        P(),
        P("pipe", None),
        P("pipe", None, None),
        P("pipe", None, None),
        P("pipe", None, None, None),
        P("pipe", None),
        P("pipe", None, None),
        P("pipe", "seq", None),
    )
    out_specs = P("pipe", "seq", None)
    return jax.shard_map(local, mesh=mesh, in_specs=in_specs, out_specs=out_specs, check_vma=False)
```
